512 devices in a mesh: row: 64 (over z, x_lo, core), col: 8 (over y, x_hi).
Axes of the slice: x: 4 (x_hi: 2, x_lo: 2; x = x_hi * 2 + x_lo), y: 4, z: 16, core: 2. Of those that a mesh axis runs over, the one named last changes fastest.
Arguments:
- features: bfloat16 [49152, 512], P(('row', 'col')), may hold values from -6 to 6
- degree: int32 [49152], P(('row', 'col')), may hold values from 1 to 32
- w_self: bfloat16 [512, 512], replicated, may hold values from -0.25 to 0.25
- w_neigh: bfloat16 [512, 512], replicated, may hold values from -0.25 to 0.25
- bias_term: float32 [512], replicated, may hold values from -4 to 4
- tile_index: int32 [64, 8, 72, 3], P('row', 'col'), may hold values from 0 to 64, as said below
- tile_edges: int32 [64, 8, 72, 64], P('row', 'col'), may hold values from 0 to 16383, as said below
- old_grad: bfloat16 [49152, 512], P(('row', 'col')), may hold values from -6 to 6
- old_degree: int32 [49152], P(('row', 'col')), may hold values from 1 to 32
- old_index: int32 [64, 8, 72, 3], P('row', 'col'), may hold values from 0 to 64, as said below
- old_edges: int32 [64, 8, 72, 64], P('row', 'col'), may hold values from 0 to 16383, as said below
Outputs:
- output: bfloat16 [49152, 512], P(('row', 'col'))
- grad_input: bfloat16 [49152, 512], P(('row', 'col'))
The draws below stay inside these ranges and needn't reach their ends.
Inputs may be any that keep to these rules, and one draw needn't show every extreme that they name: `tile_index`: each slot holds a row block under 6, a column block under 48 and an edge count of 0 to 64; on each device slots with a positive count come first; one device has all 72 slots live; every device has a slot with 64 edges. Row and column blocks may repeat. `tile_edges`: each entry is target * 128 + source inside its tile. `old_index`: as for tile_index. `old_edges`: as for tile_edges.
All inputs are finite; a program needn't handle non-finite values.
Results may differ from the reference program's by a relative error of at most 0.01.
Values may be sent and summed in bfloat16 or wider, within the bound.
No kernel may reach another device: no remote copies, remote signals or barrier semaphores. Data moves between devices by JAX's collectives and lax.ppermute only.
A program may use at most 128 MiB of HBM per device.

```python
import jax
import jax.numpy as jnp
from jax import lax

ND = 96
F = 512
TILE = 128
EPT = 64
PROWS = 64
PCOLS = 8
NODES = 49152
TILES = 72
RTILES = 6
CTILES = 48


def graph_slots(key):
    key_live, key_row, key_col, key_count, key_full, key_top = jax.random.split(key, 6)
    devices = PROWS * PCOLS
    halvings = jax.random.randint(key_live, (PROWS, PCOLS), 0, 4)
    full_device = jax.random.randint(key_full, (), 0, devices)
    flat_ids = jnp.arange(devices, dtype=jnp.int32).reshape(PROWS, PCOLS)
    halvings = jnp.where(flat_ids == full_device, 0, halvings)
    live_slots = jnp.right_shift(jnp.int32(TILES), halvings)
    slot_ids = jnp.arange(TILES, dtype=jnp.int32)
    is_live = slot_ids[None, None, :] < live_slots[:, :, None]
    counts = jax.random.randint(key_count, (PROWS, PCOLS, TILES), 1, EPT + 1)
    top_slot = jax.random.randint(key_top, (PROWS, PCOLS), 0, live_slots)
    counts = jnp.where(slot_ids[None, None, :] == top_slot[:, :, None], EPT, counts)
    counts = jnp.where(is_live, counts, 0)
    row_block = jax.random.randint(key_row, (PROWS, PCOLS, TILES), 0, RTILES)
    col_block = jax.random.randint(key_col, (PROWS, PCOLS, TILES), 0, CTILES)
    return jnp.stack([row_block, col_block, counts], axis=-1).astype(jnp.int32)


def draw_tile_index(key, part):
    key = jax.random.fold_in(key, 11)
    return graph_slots(key)


def draw_tile_edges(key, part):
    key = jax.random.fold_in(key, 12)
    return jax.random.randint(key, (PROWS, PCOLS, TILES, EPT), 0, TILE * TILE).astype(jnp.int32)


def draw_old_index(key, part):
    key = jax.random.fold_in(key, 13)
    return graph_slots(key)


def draw_old_edges(key, part):
    key = jax.random.fold_in(key, 14)
    return jax.random.randint(key, (PROWS, PCOLS, TILES, EPT), 0, TILE * TILE).astype(jnp.int32)


def place_ends(values, own_key, low, high):
    index_at = [jax.random.randint(jax.random.fold_in(own_key, axis), (), 0, length) for axis, length in enumerate(values.shape)]
    longest = values.shape.index(max(values.shape))
    neighbour = index_at[:longest] + [(index_at[longest] + 1) % values.shape[longest]] + index_at[longest + 1:]
    return values.at[tuple(index_at)].set(low).at[tuple(neighbour)].set(high)


def level_of(rng, dims, shards, smallest, top_value):
    gain, own = 1.0, jax.random.fold_in(rng, 6)
    for dim, blocks in shards:
        steps = jnp.exp(jax.random.uniform(jax.random.fold_in(own, dim), (blocks,), jnp.float32, smallest / len(shards), top_value / len(shards)))
        gain = gain * jnp.repeat(steps, dims[dim] // blocks).reshape([-1 if axis == dim else 1 for axis in range(len(dims))])
    return gain


def scatter_about(stream_key, shape, spread, reach, pieces=(), kind=jnp.bfloat16):
    values = jax.random.normal(stream_key, shape, jnp.float32) * spread
    if len(pieces) > 0:
        values = level_of(stream_key, shape, pieces, -0.22, 0.18) * values
    return jnp.clip(values, min=-reach, max=reach).astype(kind)


def setup_inputs(seed: int = 0) -> dict:
    seeds = jax.random.split(jax.random.key(seed), 12)
    features = scatter_about(seeds[0], (NODES, F), 1.0, 6.0, ((0, 512),))
    degree = place_ends(jax.random.randint(seeds[1], (NODES,), 1, 33), jax.random.fold_in(seeds[1], 1), 1, 32).astype(jnp.int32)
    w_self = scatter_about(seeds[2], (F, F), F ** -0.5, 0.25)
    w_neigh = scatter_about(seeds[3], (F, F), F ** -0.5, 0.25)
    bias_term = scatter_about(seeds[4], (F,), 1.0, 4.0, (), jnp.float32)
    tile_index = draw_tile_index(jax.random.fold_in(seeds[11], 71), 0)
    tile_edges = draw_tile_edges(jax.random.fold_in(seeds[11], 71), 0)
    old_grad = scatter_about(seeds[7], (NODES, F), 1.0, 6.0, ((0, 512),))
    old_degree = place_ends(jax.random.randint(seeds[8], (NODES,), 1, 33), jax.random.fold_in(seeds[8], 1), 1, 32).astype(jnp.int32)
    old_index = draw_old_index(jax.random.fold_in(seeds[11], 71), 0)
    old_edges = draw_old_edges(jax.random.fold_in(seeds[11], 71), 0)
    return dict(features=features, degree=degree, w_self=w_self, w_neigh=w_neigh, bias_term=bias_term, tile_index=tile_index, tile_edges=tile_edges, old_grad=old_grad, old_degree=old_degree, old_index=old_index, old_edges=old_edges)


def regroup(values):
    width = values.shape[1]
    blocks = values.reshape(PROWS, PCOLS, ND, width)
    return jnp.transpose(blocks, (1, 0, 2, 3)).reshape(PCOLS, PROWS * ND, width)


def group_sums(tile_rows, edge_rows, colsets):
    def device_sums(slot_info, slot_edges, sources):
        is_live = (jnp.arange(EPT)[None, :] < slot_info[:, 2:3]).astype(jnp.float32)
        target = (slot_info[:, 0:1] * TILE + slot_edges // TILE).reshape(-1)
        source_col = (slot_info[:, 1:2] * TILE + slot_edges % TILE).reshape(-1)
        values = sources[source_col].astype(jnp.float32) * is_live.reshape(-1, 1)
        sums = jax.ops.segment_sum(values, target, num_segments=PCOLS * ND)
        rounded = lax.optimization_barrier(sums.astype(jnp.bfloat16))
        return rounded.astype(jnp.float32)
    partials = jax.vmap(device_sums)(tile_rows, edge_rows, colsets)
    return jnp.sum(partials, axis=0)


def all_sums(tile_index, tile_edges, values):
    colsets = regroup(values)
    sums = lax.map(lambda pair: group_sums(pair[0], pair[1], colsets), (tile_index, tile_edges))
    return sums.reshape(-1, values.shape[1])


def reference(features, degree, w_self, w_neigh, bias_term, tile_index, tile_edges, old_grad, old_degree, old_index, old_edges):
    summed = all_sums(tile_index, tile_edges, features)
    neighbour_mean = (summed / degree[:, None].astype(jnp.float32)).astype(jnp.bfloat16)
    preact = jnp.dot(features, w_self, preferred_element_type=jnp.float32)
    preact = preact + jnp.dot(neighbour_mean, w_neigh, preferred_element_type=jnp.float32) + bias_term
    output = jax.nn.relu(preact).astype(jnp.bfloat16)
    mean_grad = jnp.dot(old_grad, w_neigh.T, preferred_element_type=jnp.float32)
    mean_grad = (mean_grad / old_degree[:, None].astype(jnp.float32)).astype(jnp.bfloat16)
    old_summed = all_sums(old_index, old_edges, mean_grad)
    grad_input = jnp.dot(old_grad, w_self.T, preferred_element_type=jnp.float32) + old_summed
    return output, grad_input.astype(jnp.bfloat16)
```

```python
import jax
import jax.numpy as jnp
from jax import lax
from jax.experimental import pallas as pl
from jax.experimental.pallas import tpu as pltpu
from jax.sharding import Mesh
from jax.sharding import PartitionSpec as P

TILE = 128
GROUP = 4
MIB = 1024 * 1024
PARTS = ("z", "xl", "core", "y", "xh")
PLANE = ("xl", "y", "xh")
SHIFTS = (64, 32, 16, 8, 4, 2)


def count_kernel(live_ref, place_ref, dst_ref, src_ref, out_ref, total):
    half = pl.program_id(0)
    total[...] = jnp.zeros_like(total)
    lane_ids = lax.broadcasted_iota(jnp.int32, (TILE, dst_ref.shape[2]), 0)

    def add_group(step, carry):
        slots = [step * GROUP + offset for offset in range(GROUP)]
        counts = []
        for slot in slots:
            dst_hot = (lane_ids == dst_ref[0, pl.ds(slot, 1), :]).astype(jnp.bfloat16)
            src_hot = (lane_ids == src_ref[0, pl.ds(slot, 1), :]).astype(jnp.bfloat16)
            counts.append(
                lax.dot_general(
                    dst_hot, src_hot, (((1,), (1,)), ((), ())), preferred_element_type=jnp.float32
                )
            )
        for slot, count in zip(slots, counts):
            rows = pl.ds(pl.multiple_of(place_ref[half, 0, slot] * TILE, TILE), TILE)
            total[place_ref[half, 1, slot], rows, :] += count
        return carry

    lax.fori_loop(0, pl.cdiv(live_ref[half], GROUP), add_group, 0)
    for block in range(total.shape[0]):
        out_ref[:, block * TILE : (block + 1) * TILE] = total[block].astype(jnp.bfloat16)


def edge_counts(live, place, dst, src, rows, depth):
    halves, slots, width = dst.shape
    blocks = depth // TILE
    return pl.pallas_call(
        count_kernel,
        out_shape=jax.ShapeDtypeStruct((halves * rows, depth), jnp.bfloat16),
        grid_spec=pltpu.PrefetchScalarGridSpec(
            num_scalar_prefetch=2,
            grid=(halves,),
            in_specs=[pl.BlockSpec((1, slots, width), lambda h, *_: (h, 0, 0))] * 2,
            out_specs=pl.BlockSpec((rows, depth), lambda h, *_: (h, 0)),
            scratch_shapes=[pltpu.VMEM((blocks, rows, TILE), jnp.float32)],
        ),
        compiler_params=pltpu.CompilerParams(vmem_limit_bytes=40 * MIB),
        cost_estimate=pl.CostEstimate(
            flops=2 * 10**9, bytes_accessed=40 * 10**6, transcendentals=0
        ),
    )(live, place, dst, src)


def product_kernel(place_ref, counts_ref, sources_ref, out_ref, held):
    @pl.when(pl.program_id(0) == 0)
    def _():
        planes = sources_ref.shape[0]
        wide = pl.ds(pl.multiple_of(place_ref[0], TILE // 2), TILE)
        narrow = pl.ds(pl.multiple_of(place_ref[1], TILE // 2), TILE // 2)
        for z in range(planes):
            held[z * TILE : (z + 1) * TILE] = sources_ref[z, wide]
            begin = planes * TILE + z * TILE // 2
            held[begin : begin + TILE // 2] = sources_ref[z, narrow]

    out_ref[...] = jnp.dot(
        counts_ref[...], held[...], preferred_element_type=jnp.float32
    ).astype(jnp.bfloat16)


def edge_products(place, counts, sources, chunk=512):
    rows, depth = counts.shape
    planes, height, width = sources.shape
    return pl.pallas_call(
        product_kernel,
        out_shape=jax.ShapeDtypeStruct((rows, width), jnp.bfloat16),
        grid_spec=pltpu.PrefetchScalarGridSpec(
            num_scalar_prefetch=1,
            grid=(rows // chunk,),
            in_specs=[
                pl.BlockSpec((chunk, depth), lambda m, *_: (m, 0)),
                pl.BlockSpec((planes, height, width), lambda m, *_: (0, 0, 0)),
            ],
            out_specs=pl.BlockSpec((chunk, width), lambda m, *_: (m, 0)),
            scratch_shapes=[pltpu.VMEM((depth, width), jnp.bfloat16)],
        ),
        compiler_params=pltpu.CompilerParams(vmem_limit_bytes=40 * MIB),
        cost_estimate=pl.CostEstimate(
            flops=2 * rows * depth * width, bytes_accessed=30 * 10**6, transcendentals=0
        ),
    )(place, counts, sources)


def slot_plan(index, edges, lane, planes):
    plane, part = index[..., 1] // 3, index[..., 1] % 3
    whole = part == 2 * lane
    source = edges % TILE
    own = whole[..., None] | ((part == 1)[..., None] & (source // (TILE // 2) == lane))
    own &= lax.iota(jnp.int32, edges.shape[-1]) < index[..., 2:3]
    in_half = source % (TILE // 2) + (plane % 2)[..., None] * (TILE // 2)
    src = jnp.where(own, jnp.where(whole[..., None], source, in_half), -1)
    block = jnp.where(whole, plane, planes + plane // 2)
    live = jnp.sum((index[..., 2] > 0).astype(jnp.int32), axis=-1)
    place = jnp.stack([index[..., 0], block], axis=-2)
    return live, place, edges // TILE, src


def gather_scaled(values):
    top = jnp.max(jnp.abs(values)).astype(jnp.float32)
    scale = jnp.float32(1)
    flags = []
    for shift in SHIFTS:
        fits = top * 2.0**shift <= 2.0**15
        top = jnp.where(fits, top * 2.0**shift, top)
        scale = jnp.where(fits, scale * 2.0**shift, scale)
        flags.append(fits.astype(jnp.float16))
    nodes, width = values.shape
    lane_ids = lax.broadcasted_iota(jnp.int32, (8, width), 1)
    tail = jnp.zeros((8, width), jnp.float16)
    for place, flag in enumerate(flags):
        tail = jnp.where(lane_ids == place, flag, tail)
    sent = (values.astype(jnp.float32) * scale).astype(jnp.float16)
    sent = jnp.concatenate([sent, tail], axis=0)
    got = lax.all_gather(sent, ("z", "core"), axis=0, tiled=False)
    undo = jnp.ones((got.shape[0], 1, 1), jnp.float32)
    for place, shift in enumerate(SHIFTS):
        undo = undo * jnp.where(got[:, nodes : nodes + 1, place : place + 1] > 0, 2.0**-shift, 1.0)
    got = (got[:, :nodes].astype(jnp.float32) * undo).astype(jnp.bfloat16)
    return got.reshape(-1, 2 * nodes, width)


def shards(
    features,
    degree,
    w_self,
    w_neigh,
    bias_term,
    tile_index,
    tile_edges,
    old_grad,
    old_degree,
    old_index,
    old_edges,
):
    nodes, width = features.shape
    planes = lax.axis_size("z")
    depth = 2 * planes * nodes
    rows = lax.axis_size("y") * lax.axis_size("xh") * nodes
    lane = lax.axis_index("xl")

    all_features = lax.all_gather(features, ("z", "core"), axis=0, tiled=True)
    all_features = all_features.reshape(planes, 2 * nodes, width)

    mean_grad = lax.dot_general(
        old_grad, w_neigh, (((1,), (1,)), ((), ())), preferred_element_type=jnp.float32
    )
    mean_grad = (mean_grad / old_degree[:, None].astype(jnp.float32)).astype(jnp.bfloat16)

    own_slots = jnp.stack(
        [
            jnp.concatenate([tile_index[0, 0], tile_edges[0, 0]], axis=1),
            jnp.concatenate([old_index[0, 0], old_edges[0, 0]], axis=1),
        ]
    )
    other_slots = lax.ppermute(own_slots, "xl", [(0, 1), (1, 0)])
    pair = jnp.stack(
        [
            jnp.where(lane == 0, own_slots, other_slots),
            jnp.where(lane == 0, other_slots, own_slots),
        ],
        axis=1,
    )
    place = jnp.stack([lane * (TILE // 2), (1 - lane) * TILE])
    new_plan = slot_plan(pair[0, :, :, :3], pair[0, :, :, 3:], lane, planes)
    old_plan = slot_plan(pair[1, :, :, :3], pair[1, :, :, 3:], lane, planes)

    all_grads = gather_scaled(mean_grad)

    def partial_sums(plan, sources):
        counts = edge_counts(*plan, rows, depth)
        partial = edge_products(place, counts, sources)
        return lax.all_to_all(partial.reshape(-1, nodes, width), PLANE, 0, 0)

    old_parts = partial_sums(old_plan, all_grads)
    new_parts = partial_sums(new_plan, all_features)

    old_summed = jnp.sum(old_parts.astype(jnp.float32), axis=0)
    self_grad = lax.dot_general(
        old_grad, w_self, (((1,), (1,)), ((), ())), preferred_element_type=jnp.float32
    )
    grad_input = (self_grad + old_summed).astype(jnp.bfloat16)

    summed = jnp.sum(new_parts.astype(jnp.float32), axis=0)
    neighbour_mean = (summed / degree[:, None].astype(jnp.float32)).astype(jnp.bfloat16)
    preact = jnp.dot(features, w_self, preferred_element_type=jnp.float32) + bias_term
    preact = preact + jnp.dot(neighbour_mean, w_neigh, preferred_element_type=jnp.float32)
    output = jax.nn.relu(preact).astype(jnp.bfloat16)
    return (output, grad_input)


def solution(mesh):
    devices = mesh.devices.reshape(16, 2, 2, 4, 2)
    parts = Mesh(devices, PARTS)
    block = ("z", "xl", "core")
    side = ("y", "xh")
    in_specs = (
        P(PARTS, None),
        P(PARTS),
        P(),
        P(),
        P(),
        P(block, side, None, None),
        P(block, side, None, None),
        P(PARTS, None),
        P(PARTS),
        P(block, side, None, None),
        P(block, side, None, None),
    )
    out_specs = (P(PARTS, None), P(PARTS, None))
    return jax.shard_map(
        shards, mesh=parts, in_specs=in_specs, out_specs=out_specs, check_vma=False
    )
```

```python
import jax
import jax.numpy as jnp
from jax import lax
from jax.experimental import pallas as pl
from jax.experimental.pallas import tpu as pltpu
from jax.sharding import Mesh
from jax.sharding import PartitionSpec as P

TILE = 128
HALF = TILE // 2
UNROLL = 12
EXACT = 256
MIB = 1024 * 1024
PARTS = ("z", "xl", "core", "y", "xh")
PLANE = ("xl", "y", "xh")
SHIFTS = (64, 32, 16, 8, 4, 2)


def column_of(row):
    count = row.shape[1]
    across = lax.broadcasted_iota(jnp.int32, (count, count), 0)
    down = lax.broadcasted_iota(jnp.int32, (count, count), 1)
    return jnp.sum(jnp.where(across == down, row, 0.0), axis=1, keepdims=True)


def scaled(values):
    top = jnp.max(jnp.max(jnp.abs(values), axis=1, keepdims=True), axis=0, keepdims=True)
    scale = jnp.ones_like(top)
    flags = []
    for shift in SHIFTS:
        fits = top * 2.0**shift <= 2.0**15
        factor = jnp.where(fits, 2.0**shift, 1.0)
        top, scale = top * factor, scale * factor
        flags.append(jnp.where(fits, 1.0, 0.0))
    return values * scale, flags


def prepare_kernel(
    features_ref,
    grad_ref,
    weight_ref,
    degree_ref,
    index_ref,
    edges_ref,
    old_index_ref,
    old_edges_ref,
    sent_ref,
    slots_ref,
):
    nodes, width = grad_ref.shape
    for at, (index, edges) in enumerate(
        ((index_ref, edges_ref), (old_index_ref, old_edges_ref))
    ):
        slots, fields = index.shape
        numbers = index[...].astype(jnp.float32)
        lanes = lax.broadcasted_iota(jnp.int32, (slots, TILE), 1)
        row = jnp.zeros((slots, TILE), jnp.float32)
        for field in range(fields):
            row = jnp.where(lanes == HALF + field, numbers[:, field : field + 1], row)
        slots_ref[at, :slots, :] = row.astype(jnp.int32)
        slots_ref[at, :slots, :HALF] = edges[...]
        wide = jnp.concatenate([row, jnp.zeros((TILE - slots, TILE), jnp.float32)], axis=0)
        slots_ref[at, slots:, :] = wide.T[HALF : HALF + 8, :].astype(jnp.int32)

    product = lax.dot_general(
        grad_ref[...],
        weight_ref[...],
        (((1,), (1,)), ((), ())),
        preferred_element_type=jnp.float32,
    )
    degree = column_of(degree_ref[...].astype(jnp.float32))
    mean_grad = (product / degree).astype(jnp.bfloat16).astype(jnp.float32)
    values, flags = scaled(mean_grad)
    sent_ref[:nodes, :] = values
    values, more = scaled(features_ref[...].astype(jnp.float32))
    sent_ref[nodes : 2 * nodes, :] = values
    lanes = lax.broadcasted_iota(jnp.int32, (8, width), 1)
    tail = jnp.zeros((8, width), jnp.float32)
    for at, flag in enumerate(flags + more):
        tail = jnp.where(lanes == at, flag, tail)
    sent_ref[2 * nodes :, :] = tail


def prepare(features, old_grad, w_neigh, old_degree, tables):
    nodes, width = features.shape
    slots = tables[0].shape[0]
    return pl.pallas_call(
        prepare_kernel,
        out_shape=(
            jax.ShapeDtypeStruct((2 * nodes + 8, width), jnp.float32),
            jax.ShapeDtypeStruct((2, slots + 8, TILE), jnp.int32),
        ),
        compiler_params=pltpu.CompilerParams(vmem_limit_bytes=8 * MIB),
    )(features, old_grad, w_neigh, old_degree, *tables)


def sums_kernel(
    lane_ref,
    own_info,
    other_info,
    own_ref,
    other_ref,
    sources_ref,
    out_ref,
    edges,
    dst_rows,
    src_rows,
    counts,
    held,
    total,
    sems,
):
    step = pl.program_id(0)
    lane = lane_ref[0]
    planes = sources_ref.shape[0]
    pairs = dst_rows.shape[0]

    def fetch(plane):
        whole = pltpu.make_async_copy(
            sources_ref.at[plane, pl.ds(pl.multiple_of(lane * HALF, HALF), TILE)],
            held.at[pl.ds(plane * TILE, TILE)],
            sems.at[plane],
        )
        part = pltpu.make_async_copy(
            sources_ref.at[plane, pl.ds(pl.multiple_of((1 - lane) * TILE, HALF), HALF)],
            held.at[pl.ds(planes * TILE + plane * HALF, HALF)],
            sems.at[planes + plane],
        )
        return whole, part

    @pl.when(step == 0)
    def _():
        for plane in range(planes):
            for copy in fetch(plane):
                copy.start()
        edges[...] = own_ref[...]

    @pl.when(step == 1)
    def _():
        edges[...] = other_ref[...]

    lanes = lax.broadcasted_iota(jnp.int32, (pairs, TILE), 1)
    left = lanes < HALF
    even, odd = edges[pl.ds(0, pairs, 2), :], edges[pl.ds(1, pairs, 2), :]

    def field(at):
        return jnp.where(left, even[:, at : at + 1], odd[:, at : at + 1])

    values = jnp.where(left, even, pltpu.roll(odd, HALF, 1))
    column, count = field(HALF + 1), field(HALF + 2)
    plane = (column * 43) >> 7
    part = column - 3 * plane
    source = values & (TILE - 1)
    whole = part == 2 * lane
    own = whole | ((part == 1) & ((source >> 6) == lane))
    own &= (lanes & (HALF - 1)) < count
    place = jnp.where(whole, source, (source & (HALF - 1)) + (plane & 1) * HALF)
    place += jnp.where(left, 0, TILE)
    dst_rows[...] = jnp.where(own, values >> 7, -1).astype(jnp.float32)
    src_rows[...] = jnp.where(own, place, -1).astype(jnp.float32)
    live_pairs = jnp.sum((even[:, HALF + 2 : HALF + 3] > 0).astype(jnp.int32))

    dst_ids = lax.broadcasted_iota(jnp.int32, (TILE, TILE), 0).astype(jnp.bfloat16)
    src_ids = lax.broadcasted_iota(jnp.int32, (2 * TILE, TILE), 0).astype(jnp.bfloat16)
    zero, unit = jnp.bfloat16(0), jnp.bfloat16(1)

    def spot(slot):
        row, column = [
            jnp.where(step == 0, own_info[at, slot], other_info[at, slot]) for at in (0, 1)
        ]
        plane = (column * 43) >> 7
        block = jnp.where(column - 3 * plane == 2 * lane, plane, planes + (plane >> 1))
        return block, pl.ds(pl.multiple_of(row * TILE, TILE), TILE)

    def pair_counts(pair):
        dst = dst_rows[pl.ds(pair, 1), :].astype(jnp.bfloat16)
        src = src_rows[pl.ds(pair, 1), :].astype(jnp.bfloat16)
        dst_hot = jnp.where(dst_ids == dst, unit, zero)
        src_hot = jnp.where(src_ids == src, unit, zero)
        return lax.dot_general(
            dst_hot, src_hot, (((1,), (1,)), ((), ())), preferred_element_type=jnp.float32
        ).astype(jnp.bfloat16)

    def build(first, last, unroll):
        counts[...] = jnp.zeros_like(counts)

        def add(turn, peak):
            found = [first + turn * unroll + at for at in range(unroll)]
            added = [pair_counts(pair) for pair in found]
            for pair, both in zip(found, added):
                for side in range(2):
                    block, rows = spot(2 * pair + side)
                    sums = counts[block, rows, :] + both[:, side * TILE : (side + 1) * TILE]
                    counts[block, rows, :] = sums
                    peak = jnp.maximum(peak, sums)
            return peak

        start = jnp.zeros((TILE, TILE), jnp.bfloat16)
        return lax.fori_loop(0, pl.cdiv(last - first, unroll), add, start)

    def product():
        left_side = jnp.concatenate([counts[at] for at in range(counts.shape[0])], axis=1)
        return jnp.dot(left_side, held[...], preferred_element_type=jnp.float32)

    peak = jnp.max(build(0, live_pairs, UNROLL).astype(jnp.float32))

    @pl.when(step == 0)
    def _():
        for plane in range(planes):
            for copy in fetch(plane):
                copy.wait()

    @pl.when(peak < EXACT)
    def _():
        out_ref[...] = product().astype(jnp.bfloat16)

    @pl.when(peak >= EXACT)
    def _():
        total[...] = jnp.zeros_like(total)

        def some(turn, carry):
            build(2 * turn, 2 * turn + 2, 2)
            total[...] += product()
            return carry

        lax.fori_loop(0, pairs // 2, some, 0)
        out_ref[...] = total[...].astype(jnp.bfloat16)


def edge_sums(lane, own, other, which, sources, rows):
    slots = own.shape[1] - 8
    planes, height, width = sources.shape
    depth = planes * height
    table = pl.BlockSpec((None, slots, TILE), lambda step, _: (which, 0, 0))
    info = pl.BlockSpec(
        (None, 8, TILE), lambda step, _: (which, slots // 8, 0), memory_space=pltpu.SMEM
    )
    return pl.pallas_call(
        sums_kernel,
        out_shape=jax.ShapeDtypeStruct((2 * rows, width), jnp.bfloat16),
        grid_spec=pltpu.PrefetchScalarGridSpec(
            num_scalar_prefetch=1,
            grid=(2,),
            in_specs=[info, info, table, table, pl.BlockSpec(memory_space=pltpu.HBM)],
            out_specs=pl.BlockSpec(
                (rows, width), lambda step, lane: (step + lane[0] - 2 * step * lane[0], 0)
            ),
            scratch_shapes=[
                pltpu.VMEM((slots, TILE), jnp.int32),
                pltpu.VMEM((slots // 2, TILE), jnp.float32),
                pltpu.VMEM((slots // 2, TILE), jnp.float32),
                pltpu.VMEM((depth // TILE, rows, TILE), jnp.bfloat16),
                pltpu.VMEM((depth, width), jnp.bfloat16),
                pltpu.VMEM((rows, width), jnp.float32),
                pltpu.SemaphoreType.DMA((2 * planes,)),
            ],
        ),
        compiler_params=pltpu.CompilerParams(vmem_limit_bytes=28 * MIB),
        cost_estimate=pl.CostEstimate(
            flops=8 * 10**9, bytes_accessed=10 * 10**6, transcendentals=0
        ),
    )(lane, own, other, own, other, sources)


def shards(
    features,
    degree,
    w_self,
    w_neigh,
    bias_term,
    tile_index,
    tile_edges,
    old_grad,
    old_degree,
    old_index,
    old_edges,
):
    nodes, width = features.shape
    rows = lax.axis_size("y") * lax.axis_size("xh") * nodes
    lane = lax.axis_index("xl")

    tables = [table[0, 0] for table in (tile_index, tile_edges, old_index, old_edges)]
    sent, own = prepare(features, old_grad, w_neigh, old_degree[None], tables)
    other = lax.ppermute(own, "xl", [(0, 1), (1, 0)])

    got = lax.all_gather(sent.astype(jnp.float16), ("z", "core"), axis=0, tiled=False)
    flags = got[:, 2 * nodes, : 2 * len(SHIFTS)].reshape(-1, 2, len(SHIFTS))
    factors = jnp.array([2.0**-shift for shift in SHIFTS], jnp.float32)
    undo = jnp.prod(jnp.where(flags > 0, factors, 1.0), axis=-1)

    def sums(at, which):
        values = got[:, at * nodes : (at + 1) * nodes].astype(jnp.float32)
        values = (values * undo[:, at, None, None]).astype(jnp.bfloat16)
        values = values.reshape(-1, 2 * nodes, width)
        partial = edge_sums(lane.reshape(1), own, other, which, values, rows)
        return lax.all_to_all(partial.reshape(-1, nodes, width), PLANE, 0, 0)

    old_parts = sums(0, 1)
    new_parts = sums(1, 0)

    old_summed = jnp.sum(old_parts.astype(jnp.float32), axis=0)
    self_grad = lax.dot_general(
        old_grad, w_self, (((1,), (1,)), ((), ())), preferred_element_type=jnp.float32
    )
    grad_input = (self_grad + old_summed).astype(jnp.bfloat16)

    summed = jnp.sum(new_parts.astype(jnp.float32), axis=0)
    neighbour_mean = (summed / degree[:, None].astype(jnp.float32)).astype(jnp.bfloat16)
    preact = jnp.dot(features, w_self, preferred_element_type=jnp.float32) + bias_term
    preact = preact + jnp.dot(neighbour_mean, w_neigh, preferred_element_type=jnp.float32)
    output = jax.nn.relu(preact).astype(jnp.bfloat16)
    return (output, grad_input)


def solution(mesh):
    parts = Mesh(mesh.devices.reshape(16, 2, 2, 4, 2), PARTS)
    block = ("z", "xl", "core")
    side = ("y", "xh")
    in_specs = (
        P(PARTS, None),
        P(PARTS),
        P(),
        P(),
        P(),
        P(block, side, None, None),
        P(block, side, None, None),
        P(PARTS, None),
        P(PARTS),
        P(block, side, None, None),
        P(block, side, None, None),
    )
    out_specs = (P(PARTS, None), P(PARTS, None))
    return jax.shard_map(
        shards, mesh=parts, in_specs=in_specs, out_specs=out_specs, check_vma=False
    )
```

```python
import jax
import jax.numpy as jnp
from jax import lax
from jax.experimental import pallas as pl
from jax.experimental.pallas import tpu as pltpu
from jax.sharding import Mesh
from jax.sharding import PartitionSpec as P

TILE = 128
HALF = TILE // 2
UNROLL = 12
EXACT = 256
VMEM = 58 * 1024 * 1024
PARTS = ("z", "xl", "core", "y", "xh")
PLANE = ("xl", "y", "xh")
SHIFTS = (64, 32, 16, 8, 4, 2)


def column_of(row):
    count = row.shape[1]
    across = lax.broadcasted_iota(jnp.int32, (count, count), 0)
    down = lax.broadcasted_iota(jnp.int32, (count, count), 1)
    return jnp.sum(jnp.where(across == down, row, 0.0), axis=1, keepdims=True)


def scaled(values):
    top = jnp.max(jnp.max(jnp.abs(values), axis=1, keepdims=True), axis=0, keepdims=True)
    scale = jnp.ones_like(top)
    flags = []
    for shift in SHIFTS:
        fits = top * 2.0**shift <= 2.0**15
        factor = jnp.where(fits, 2.0**shift, 1.0)
        top, scale = top * factor, scale * factor
        flags.append(jnp.where(fits, 1.0, 0.0))
    return values * scale, flags


def prepare_kernel(
    features_ref,
    grad_ref,
    weight_ref,
    degree_ref,
    index_ref,
    edges_ref,
    old_index_ref,
    old_edges_ref,
    sent_ref,
    slots_ref,
):
    nodes, width = grad_ref.shape
    for at, (index, edges) in enumerate(
        ((index_ref, edges_ref), (old_index_ref, old_edges_ref))
    ):
        fields, _, slots = index.shape
        numbers = jnp.concatenate([edges[...]] + [index[field] for field in range(fields)], axis=0)
        numbers = jnp.concatenate(
            [numbers, jnp.zeros((TILE - HALF - fields, slots), jnp.int32)], axis=0
        )
        numbers = jnp.concatenate(
            [numbers, jnp.zeros((TILE, TILE - slots), jnp.int32)], axis=1
        )
        slots_ref[at, :slots, :] = numbers.astype(jnp.float32).T[:slots].astype(jnp.int32)
        slots_ref[at, slots:, :] = numbers[HALF : HALF + 8, :]

    product = lax.dot_general(
        grad_ref[...],
        weight_ref[...],
        (((1,), (1,)), ((), ())),
        preferred_element_type=jnp.float32,
    )
    degree = column_of(degree_ref[...].astype(jnp.float32))
    mean_grad = (product / degree).astype(jnp.bfloat16).astype(jnp.float32)
    values, flags = scaled(mean_grad)
    sent_ref[:nodes, :] = values
    values, more = scaled(features_ref[...].astype(jnp.float32))
    sent_ref[nodes : 2 * nodes, :] = values
    lanes = lax.broadcasted_iota(jnp.int32, (8, width), 1)
    tail = jnp.zeros((8, width), jnp.float32)
    for at, flag in enumerate(flags + more):
        tail = jnp.where(lanes == at, flag, tail)
    sent_ref[2 * nodes :, :] = tail


def prepare(features, old_grad, w_neigh, old_degree, tables):
    nodes, width = features.shape
    slots = tables[0].shape[-1]
    args = (features, old_grad, w_neigh, old_degree, *tables)
    outs = (
        jax.ShapeDtypeStruct((2 * nodes + 8, width), jnp.float32),
        jax.ShapeDtypeStruct((2, slots + 8, TILE), jnp.int32),
    )

    def whole(arg):
        return pl.BlockSpec(arg.shape, lambda _: (0,) * len(arg.shape))

    return pl.pallas_call(
        prepare_kernel,
        out_shape=outs,
        grid=(1,),
        in_specs=[whole(arg) for arg in args],
        out_specs=tuple(whole(out) for out in outs),
        compiler_params=pltpu.CompilerParams(vmem_limit_bytes=VMEM),
    )(*args)


def sums_kernel(
    lane_ref,
    own_info,
    other_info,
    own_ref,
    other_ref,
    grads_ref,
    features_ref,
    out_ref,
    edges,
    dst_rows,
    src_rows,
    counts,
    held,
    total,
    sems,
):
    array, half = pl.program_id(0), pl.program_id(1)
    lane = lane_ref[0]
    planes = grads_ref.shape[0]
    pairs = dst_rows.shape[0]

    def fetches(sources_ref, into):
        for plane in range(planes):
            yield pltpu.make_async_copy(
                sources_ref.at[plane, pl.ds(pl.multiple_of(lane * HALF, HALF), TILE)],
                held.at[into, pl.ds(plane * TILE, TILE)],
                sems.at[into, plane],
            )
            yield pltpu.make_async_copy(
                sources_ref.at[plane, pl.ds(pl.multiple_of((1 - lane) * TILE, HALF), HALF)],
                held.at[into, pl.ds(planes * TILE + plane * HALF, HALF)],
                sems.at[into, planes + plane],
            )

    @pl.when((array == 0) & (half == 0))
    def _():
        for copy in fetches(grads_ref, 0):
            copy.start()
        for copy in fetches(features_ref, 1):
            copy.start()

    @pl.when(half == 0)
    def _():
        edges[...] = own_ref[...]

    @pl.when(half == 1)
    def _():
        edges[...] = other_ref[...]

    lanes = lax.broadcasted_iota(jnp.int32, (pairs, TILE), 1)
    left = lanes < HALF
    even, odd = edges[pl.ds(0, pairs, 2), :], edges[pl.ds(1, pairs, 2), :]

    def field(at):
        return jnp.where(left, even[:, at : at + 1], odd[:, at : at + 1])

    values = jnp.where(left, even, pltpu.roll(odd, HALF, 1))
    column, count = field(HALF + 1), field(HALF + 2)
    plane = (column * 43) >> 7
    part = column - 3 * plane
    source = values & (TILE - 1)
    whole = part == 2 * lane
    own = whole | ((part == 1) & ((source >> 6) == lane))
    own &= (lanes & (HALF - 1)) < count
    place = jnp.where(whole, source, (source & (HALF - 1)) + (plane & 1) * HALF)
    place += jnp.where(left, 0, TILE)
    dst_rows[...] = jnp.where(own, values >> 7, -1).astype(jnp.float32)
    src_rows[...] = jnp.where(own, place, -1).astype(jnp.float32)
    live_pairs = jnp.sum((even[:, HALF + 2 : HALF + 3] > 0).astype(jnp.int32))

    dst_ids = lax.broadcasted_iota(jnp.int32, (TILE, TILE), 0).astype(jnp.bfloat16)
    src_ids = lax.broadcasted_iota(jnp.int32, (2 * TILE, TILE), 0).astype(jnp.bfloat16)
    zero, unit = jnp.bfloat16(0), jnp.bfloat16(1)

    def spot(slot):
        row, column = [
            jnp.where(half == 0, own_info[at, slot], other_info[at, slot]) for at in (0, 1)
        ]
        plane = (column * 43) >> 7
        block = jnp.where(column - 3 * plane == 2 * lane, plane, planes + (plane >> 1))
        return block, pl.ds(pl.multiple_of(row * TILE, TILE), TILE)

    def pair_counts(pair):
        dst = dst_rows[pl.ds(pair, 1), :].astype(jnp.bfloat16)
        src = src_rows[pl.ds(pair, 1), :].astype(jnp.bfloat16)
        dst_hot = jnp.where(dst_ids == dst, unit, zero)
        src_hot = jnp.where(src_ids == src, unit, zero)
        return lax.dot_general(
            dst_hot, src_hot, (((1,), (1,)), ((), ())), preferred_element_type=jnp.float32
        ).astype(jnp.bfloat16)

    def build(first, last, unroll):
        counts[...] = jnp.zeros_like(counts)

        def add(turn, peak):
            found = [first + turn * unroll + at for at in range(unroll)]
            added = [pair_counts(pair) for pair in found]
            for pair, both in zip(found, added):
                for side in range(2):
                    block, rows = spot(2 * pair + side)
                    sums = counts[block, rows, :] + both[:, side * TILE : (side + 1) * TILE]
                    counts[block, rows, :] = sums
                    peak = jnp.maximum(peak, sums)
            return peak

        start = jnp.zeros((TILE, TILE), jnp.bfloat16)
        return lax.fori_loop(0, pl.cdiv(last - first, unroll), add, start)

    def product():
        left_side = jnp.concatenate([counts[at] for at in range(counts.shape[0])], axis=1)
        return jnp.dot(left_side, held[array], preferred_element_type=jnp.float32)

    peak = jnp.max(build(0, live_pairs, UNROLL).astype(jnp.float32))

    @pl.when((array == 0) & (half == 0))
    def _():
        for copy in fetches(grads_ref, 0):
            copy.wait()

    @pl.when((array == 1) & (half == 0))
    def _():
        for copy in fetches(features_ref, 1):
            copy.wait()

    def put(sums):
        nodes = out_ref.shape[1]
        for at in range(out_ref.shape[0]):
            out_ref[at] = sums[at * nodes : (at + 1) * nodes].astype(jnp.bfloat16)

    @pl.when(peak < EXACT)
    def _():
        put(product())

    @pl.when(peak >= EXACT)
    def _():
        total[...] = jnp.zeros_like(total)

        def some(turn, carry):
            build(2 * turn, 2 * turn + 2, 2)
            total[...] += product()
            return carry

        lax.fori_loop(0, pairs // 2, some, 0)
        put(total[...])


def edge_sums(lane, own, other, grads, features, devices, nodes):
    slots = own.shape[1] - 8
    planes, height, width = grads.shape
    depth, rows = planes * height, devices * nodes
    table = pl.BlockSpec((None, slots, TILE), lambda array, half, _: (1 - array, 0, 0))
    info = pl.BlockSpec(
        (None, 8, TILE),
        lambda array, half, _: (1 - array, slots // 8, 0),
        memory_space=pltpu.SMEM,
    )
    far = pl.BlockSpec(memory_space=pl.ANY)
    return pl.pallas_call(
        sums_kernel,
        out_shape=jax.ShapeDtypeStruct((2 * devices, 2, nodes, width), jnp.bfloat16),
        grid_spec=pltpu.PrefetchScalarGridSpec(
            num_scalar_prefetch=1,
            grid=(2, 2),
            in_specs=[info, info, table, table, far, far],
            out_specs=pl.BlockSpec(
                (devices, None, nodes, width),
                lambda array, half, lane: (half + lane[0] - 2 * half * lane[0], array, 0, 0),
            ),
            scratch_shapes=[
                pltpu.VMEM((slots, TILE), jnp.int32),
                pltpu.VMEM((slots // 2, TILE), jnp.float32),
                pltpu.VMEM((slots // 2, TILE), jnp.float32),
                pltpu.VMEM((depth // TILE, rows, TILE), jnp.bfloat16),
                pltpu.VMEM((2, depth, width), jnp.bfloat16),
                pltpu.VMEM((rows, width), jnp.float32),
                pltpu.SemaphoreType.DMA((2, 2 * planes)),
            ],
        ),
        compiler_params=pltpu.CompilerParams(vmem_limit_bytes=VMEM),
        cost_estimate=pl.CostEstimate(
            flops=16 * 10**9, bytes_accessed=20 * 10**6, transcendentals=0
        ),
    )(lane, own, other, own, other, grads, features)


def shards(
    features,
    degree,
    w_self,
    w_neigh,
    bias_term,
    tile_index,
    tile_edges,
    old_grad,
    old_degree,
    old_index,
    old_edges,
):
    nodes, width = features.shape
    devices = lax.axis_size("y") * lax.axis_size("xh")
    lane = lax.axis_index("xl")

    tables = []
    for index, edges in ((tile_index, tile_edges), (old_index, old_edges)):
        tables.append(jnp.transpose(index[0], (2, 0, 1)))
        tables.append(edges[0, 0].T)
    sent, own = prepare(features, old_grad, w_neigh, old_degree[None], tables)
    other = lax.ppermute(own, "xl", [(0, 1), (1, 0)])

    got = lax.all_gather(sent.astype(jnp.float16), ("z", "core"), axis=0, tiled=False)
    flags = got[:, 2 * nodes, : 2 * len(SHIFTS)].reshape(-1, 2, len(SHIFTS))
    factors = jnp.array([2.0**-shift for shift in SHIFTS], jnp.float32)
    undo = jnp.prod(jnp.where(flags > 0, factors, 1.0), axis=-1)

    def sources(at):
        values = got[:, at * nodes : (at + 1) * nodes].astype(jnp.float32)
        values = (values * undo[:, at, None, None]).astype(jnp.bfloat16)
        return values.reshape(-1, 2 * nodes, width)

    partial = edge_sums(lane.reshape(1), own, other, sources(0), sources(1), devices, nodes)
    parts = lax.all_to_all(partial, PLANE, 0, 0)
    old_summed = jnp.sum(parts[:, 0].astype(jnp.float32), axis=0)
    self_grad = lax.dot_general(
        old_grad, w_self, (((1,), (1,)), ((), ())), preferred_element_type=jnp.float32
    )
    grad_input = (self_grad + old_summed).astype(jnp.bfloat16)

    summed = jnp.sum(parts[:, 1].astype(jnp.float32), axis=0)
    neighbour_mean = (summed / degree[:, None].astype(jnp.float32)).astype(jnp.bfloat16)
    preact = jnp.dot(features, w_self, preferred_element_type=jnp.float32) + bias_term
    preact = preact + jnp.dot(neighbour_mean, w_neigh, preferred_element_type=jnp.float32)
    output = jax.nn.relu(preact).astype(jnp.bfloat16)
    return (output, grad_input)


def solution(mesh):
    parts = Mesh(mesh.devices.reshape(16, 2, 2, 4, 2), PARTS)
    block = ("z", "xl", "core")
    side = ("y", "xh")
    in_specs = (
        P(PARTS, None),
        P(PARTS),
        P(),
        P(),
        P(),
        P(block, side, None, None),
        P(block, side, None, None),
        P(PARTS, None),
        P(PARTS),
        P(block, side, None, None),
        P(block, side, None, None),
    )
    out_specs = (P(PARTS, None), P(PARTS, None))
    return jax.shard_map(
        shards, mesh=parts, in_specs=in_specs, out_specs=out_specs, check_vma=False
    )
```

```python
import functools

import jax
import jax.numpy as jnp
from jax import lax
from jax.experimental import pallas as pl
from jax.experimental.pallas import tpu as pltpu
from jax.sharding import Mesh
from jax.sharding import PartitionSpec as P

TILE = 128
HALF = TILE // 2
UNROLL = 12
EXACT = 256
VMEM = 58 * 1024 * 1024
PARTS = ("z", "xl", "core", "y", "xh")
PLANE = ("xl", "y", "xh")
SHIFTS = (63, 32, 16, 8, 4, 2, 1)
LARGEST = 32767.0
TAIL = 16


def column_of(row):
    count = row.shape[1]
    across = lax.broadcasted_iota(jnp.int32, (count, count), 0)
    down = lax.broadcasted_iota(jnp.int32, (count, count), 1)
    return jnp.sum(jnp.where(across == down, row, 0.0), axis=1, keepdims=True)


def row_of(column):
    count = column.shape[0]
    across = lax.broadcasted_iota(jnp.int32, (count, count), 0)
    down = lax.broadcasted_iota(jnp.int32, (count, count), 1)
    return jnp.sum(jnp.where(across == down, column, 0.0), axis=0, keepdims=True)


def scaled(values):
    top = jnp.max(jnp.abs(values), axis=1, keepdims=True)
    scale, power = jnp.ones_like(top), jnp.zeros_like(top)
    for shift in SHIFTS:
        fits = top * 2.0**shift <= LARGEST
        factor = jnp.where(fits, 2.0**shift, 1.0)
        top, scale = top * factor, scale * factor
        power += jnp.where(fits, float(shift), 0.0)
    return jnp.round(values * scale).astype(jnp.int32).astype(jnp.int16), power


def undone(power):
    factor = jnp.ones_like(power)
    for shift in SHIFTS:
        has = power >= shift
        factor = factor * jnp.where(has, 2.0**-shift, 1.0)
        power = power - jnp.where(has, float(shift), 0.0)
    return factor


def prepare_kernel(
    features_ref,
    grad_ref,
    weight_ref,
    degree_ref,
    index_ref,
    edges_ref,
    old_index_ref,
    old_edges_ref,
    sent_ref,
    slots_ref,
):
    nodes, width = grad_ref.shape
    for at, (index, edges) in enumerate(
        ((index_ref, edges_ref), (old_index_ref, old_edges_ref))
    ):
        fields, _, slots = index.shape
        numbers = jnp.concatenate([edges[...]] + [index[field] for field in range(fields)], axis=0)
        numbers = jnp.concatenate(
            [numbers, jnp.zeros((TILE - HALF - fields, slots), jnp.int32)], axis=0
        )
        numbers = jnp.concatenate(
            [numbers, jnp.zeros((TILE, TILE - slots), jnp.int32)], axis=1
        )
        slots_ref[at, :slots, :] = numbers.astype(jnp.float32).T[:slots].astype(jnp.int32)
        slots_ref[at, slots:, :] = numbers[HALF : HALF + 8, :]

    product = lax.dot_general(
        grad_ref[...],
        weight_ref[...],
        (((1,), (1,)), ((), ())),
        preferred_element_type=jnp.float32,
    )
    degree = column_of(degree_ref[...].astype(jnp.float32))
    mean_grad = (product / degree).astype(jnp.bfloat16).astype(jnp.float32)
    values, grad_power = scaled(mean_grad)
    sent_ref[:nodes, :] = values
    values, feature_power = scaled(features_ref[...].astype(jnp.float32))
    sent_ref[nodes : 2 * nodes, :] = values
    lines = lax.broadcasted_iota(jnp.int32, (TAIL, nodes), 0)
    tail = jnp.where(lines == 0, row_of(grad_power), 0.0)
    tail = jnp.where(lines == 1, row_of(feature_power), tail)
    tail = jnp.concatenate([tail, jnp.zeros((TAIL, width - nodes), jnp.float32)], axis=1)
    sent_ref[2 * nodes :, :] = tail.astype(jnp.int32).astype(jnp.int16)


def prepare(features, old_grad, w_neigh, old_degree, tables):
    nodes, width = features.shape
    slots = tables[0].shape[-1]
    args = (features, old_grad, w_neigh, old_degree, *tables)
    outs = (
        jax.ShapeDtypeStruct((2 * nodes + TAIL, width), jnp.int16),
        jax.ShapeDtypeStruct((2, slots + 8, TILE), jnp.int32),
    )

    def whole(arg):
        return pl.BlockSpec(arg.shape, lambda _: (0,) * len(arg.shape))

    return pl.pallas_call(
        prepare_kernel,
        out_shape=outs,
        grid=(1,),
        in_specs=[whole(arg) for arg in args],
        out_specs=tuple(whole(out) for out in outs),
        compiler_params=pltpu.CompilerParams(vmem_limit_bytes=VMEM),
    )(*args)


def sums_kernel(
    array,
    lane_ref,
    own_info,
    other_info,
    own_ref,
    other_ref,
    sent_ref,
    out_ref,
    edges,
    dst_rows,
    src_rows,
    counts,
    raw,
    tails,
    factors,
    held,
    total,
    sems,
):
    half = pl.program_id(0)
    lane = lane_ref[0]
    nodes = out_ref.shape[1]
    senders = tails.shape[0]
    planes = senders // 2
    pairs = dst_rows.shape[0]

    fetches = [
        pltpu.make_async_copy(
            sent_ref.at[sender, pl.ds(array * nodes, nodes)],
            raw.at[pl.ds(sender * nodes, nodes)],
            sems.at[sender],
        )
        for sender in range(senders)
    ]
    fetches.append(
        pltpu.make_async_copy(
            sent_ref.at[:, pl.ds(2 * nodes, TAIL), pl.ds(0, TILE)], tails, sems.at[senders]
        )
    )

    @pl.when(half == 0)
    def _():
        for copy in fetches:
            copy.start()
        edges[...] = own_ref[...]

    @pl.when(half == 1)
    def _():
        edges[...] = other_ref[...]

    def hold():
        powers = jnp.concatenate([tails[sender, array : array + 1, :] for sender in range(senders)], axis=0)
        factor = undone(powers.astype(jnp.int32).astype(jnp.float32))
        factor = jnp.concatenate([factor, jnp.ones((TILE - senders, TILE), jnp.float32)], axis=0).T
        for sender in range(senders):
            factors[sender * nodes : (sender + 1) * nodes] = jnp.broadcast_to(
                factor[:nodes, sender : sender + 1], (nodes, TILE)
            )

        def move(begin, into, size):
            rows = pl.ds(pl.multiple_of(begin, HALF), size)
            values = raw[rows, :].astype(jnp.int32).astype(jnp.float32)
            times = factors[rows, :]
            times = jnp.concatenate([times] * (values.shape[1] // TILE), axis=1)
            held[pl.ds(pl.multiple_of(into, HALF), size), :] = (values * times).astype(jnp.bfloat16)

        def move_plane(plane, carry):
            begin = plane * 2 * nodes
            move(begin + lane * HALF, plane * TILE, TILE)
            move(begin + (1 - lane) * TILE, planes * TILE + plane * HALF, HALF)
            return carry

        lax.fori_loop(0, planes, move_plane, 0)

    lanes = lax.broadcasted_iota(jnp.int32, (pairs, TILE), 1)
    left = lanes < HALF
    even, odd = edges[pl.ds(0, pairs, 2), :], edges[pl.ds(1, pairs, 2), :]

    def field(at):
        return jnp.where(left, even[:, at : at + 1], odd[:, at : at + 1])

    values = jnp.where(left, even, pltpu.roll(odd, HALF, 1))
    column, count = field(HALF + 1), field(HALF + 2)
    plane = (column * 43) >> 7
    part = column - 3 * plane
    source = values & (TILE - 1)
    whole = part == 2 * lane
    own = whole | ((part == 1) & ((source >> 6) == lane))
    own &= (lanes & (HALF - 1)) < count
    place = jnp.where(whole, source, (source & (HALF - 1)) + (plane & 1) * HALF)
    place += jnp.where(left, 0, TILE)
    dst_rows[...] = jnp.where(own, values >> 7, -1).astype(jnp.float32)
    src_rows[...] = jnp.where(own, place, -1).astype(jnp.float32)
    live_pairs = jnp.sum((even[:, HALF + 2 : HALF + 3] > 0).astype(jnp.int32))

    dst_ids = lax.broadcasted_iota(jnp.int32, (TILE, TILE), 0).astype(jnp.bfloat16)
    src_ids = lax.broadcasted_iota(jnp.int32, (2 * TILE, TILE), 0).astype(jnp.bfloat16)
    zero, unit = jnp.bfloat16(0), jnp.bfloat16(1)

    def spot(slot):
        row, column = [
            jnp.where(half == 0, own_info[at, slot], other_info[at, slot]) for at in (0, 1)
        ]
        plane = (column * 43) >> 7
        block = jnp.where(column - 3 * plane == 2 * lane, plane, planes + (plane >> 1))
        return block, pl.ds(pl.multiple_of(row * TILE, TILE), TILE)

    def pair_counts(pair):
        dst = dst_rows[pl.ds(pair, 1), :].astype(jnp.bfloat16)
        src = src_rows[pl.ds(pair, 1), :].astype(jnp.bfloat16)
        dst_hot = jnp.where(dst_ids == dst, unit, zero)
        src_hot = jnp.where(src_ids == src, unit, zero)
        return lax.dot_general(
            dst_hot, src_hot, (((1,), (1,)), ((), ())), preferred_element_type=jnp.float32
        ).astype(jnp.bfloat16)

    def build(first, last, unroll):
        counts[...] = jnp.zeros_like(counts)

        def add(turn, peak):
            found = [first + turn * unroll + at for at in range(unroll)]
            added = [pair_counts(pair) for pair in found]
            for pair, both in zip(found, added):
                for side in range(2):
                    block, rows = spot(2 * pair + side)
                    sums = counts[block, rows, :] + both[:, side * TILE : (side + 1) * TILE]
                    counts[block, rows, :] = sums
                    peak = jnp.maximum(peak, sums)
            return peak

        start = jnp.zeros((TILE, TILE), jnp.bfloat16)
        return lax.fori_loop(0, pl.cdiv(last - first, unroll), add, start)

    def product():
        left_side = jnp.concatenate([counts[at] for at in range(counts.shape[0])], axis=1)
        return jnp.dot(left_side, held[...], preferred_element_type=jnp.float32)

    peak = jnp.max(build(0, live_pairs, UNROLL).astype(jnp.float32))

    @pl.when(half == 0)
    def _():
        for copy in fetches:
            copy.wait()
        hold()

    def put(sums):
        for at in range(out_ref.shape[0]):
            out_ref[at] = sums[at * nodes : (at + 1) * nodes].astype(jnp.bfloat16)

    @pl.when(peak < EXACT)
    def _():
        put(product())

    @pl.when(peak >= EXACT)
    def _():
        total[...] = jnp.zeros_like(total)

        def some(turn, carry):
            build(2 * turn, 2 * turn + 2, 2)
            total[...] += product()
            return carry

        lax.fori_loop(0, pairs // 2, some, 0)
        put(total[...])


def edge_sums(array, lane, own, other, sent, devices, nodes):
    slots = own.shape[1] - 8
    senders, _, width = sent.shape
    depth, rows = senders * nodes, devices * nodes
    table = pl.BlockSpec((None, slots, TILE), lambda half, _: (1 - array, 0, 0))
    info = pl.BlockSpec(
        (None, 8, TILE), lambda half, _: (1 - array, slots // 8, 0), memory_space=pltpu.SMEM
    )
    return pl.pallas_call(
        functools.partial(sums_kernel, array),
        out_shape=jax.ShapeDtypeStruct((2 * devices, nodes, width), jnp.bfloat16),
        grid_spec=pltpu.PrefetchScalarGridSpec(
            num_scalar_prefetch=1,
            grid=(2,),
            in_specs=[info, info, table, table, pl.BlockSpec(memory_space=pl.ANY)],
            out_specs=pl.BlockSpec(
                (devices, nodes, width),
                lambda half, lane: (half + lane[0] - 2 * half * lane[0], 0, 0),
            ),
            scratch_shapes=[
                pltpu.VMEM((slots, TILE), jnp.int32),
                pltpu.VMEM((slots // 2, TILE), jnp.float32),
                pltpu.VMEM((slots // 2, TILE), jnp.float32),
                pltpu.VMEM((depth // TILE, rows, TILE), jnp.bfloat16),
                pltpu.VMEM((depth, width), jnp.int16),
                pltpu.VMEM((senders, TAIL, TILE), jnp.int16),
                pltpu.VMEM((depth, TILE), jnp.float32),
                pltpu.VMEM((depth, width), jnp.bfloat16),
                pltpu.VMEM((rows, width), jnp.float32),
                pltpu.SemaphoreType.DMA((senders + 1,)),
            ],
        ),
        compiler_params=pltpu.CompilerParams(vmem_limit_bytes=VMEM),
        cost_estimate=pl.CostEstimate(
            flops=8 * 10**9, bytes_accessed=10 * 10**6, transcendentals=0
        ),
    )(lane, own, other, own, other, sent)


def shards(
    features,
    degree,
    w_self,
    w_neigh,
    bias_term,
    tile_index,
    tile_edges,
    old_grad,
    old_degree,
    old_index,
    old_edges,
):
    nodes, width = features.shape
    devices = lax.axis_size("y") * lax.axis_size("xh")
    lane = lax.axis_index("xl")

    tables = []
    for index, edges in ((tile_index, tile_edges), (old_index, old_edges)):
        tables.append(jnp.transpose(index[0], (2, 0, 1)))
        tables.append(edges[0, 0].T)
    sent, own = prepare(features, old_grad, w_neigh, old_degree[None], tables)
    other = lax.ppermute(own, "xl", [(0, 1), (1, 0)])

    got = lax.all_gather(sent, ("z", "core"), axis=0, tiled=False)

    def sums(array):
        partial = edge_sums(array, lane.reshape(1), own, other, got, devices, nodes)
        parts = lax.all_to_all(partial, PLANE, 0, 0)
        return jnp.sum(parts.astype(jnp.float32), axis=0)

    old_summed = sums(0)
    summed = sums(1)

    self_grad = lax.dot_general(
        old_grad, w_self, (((1,), (1,)), ((), ())), preferred_element_type=jnp.float32
    )
    grad_input = (self_grad + old_summed).astype(jnp.bfloat16)

    neighbour_mean = (summed / degree[:, None].astype(jnp.float32)).astype(jnp.bfloat16)
    preact = jnp.dot(features, w_self, preferred_element_type=jnp.float32) + bias_term
    preact = preact + jnp.dot(neighbour_mean, w_neigh, preferred_element_type=jnp.float32)
    output = jax.nn.relu(preact).astype(jnp.bfloat16)
    return (output, grad_input)


def solution(mesh):
    parts = Mesh(mesh.devices.reshape(16, 2, 2, 4, 2), PARTS)
    block = ("z", "xl", "core")
    side = ("y", "xh")
    in_specs = (
        P(PARTS, None),
        P(PARTS),
        P(),
        P(),
        P(),
        P(block, side, None, None),
        P(block, side, None, None),
        P(PARTS, None),
        P(PARTS),
        P(block, side, None, None),
        P(block, side, None, None),
    )
    out_specs = (P(PARTS, None), P(PARTS, None))
    return jax.shard_map(
        shards, mesh=parts, in_specs=in_specs, out_specs=out_specs, check_vma=False
    )
```

```python
import jax
import jax.numpy as jnp
from jax import lax
from jax.experimental import pallas as pl
from jax.experimental.pallas import tpu as pltpu
from jax.sharding import Mesh
from jax.sharding import PartitionSpec as P

TILE = 128
HALF = TILE // 2
UNROLL = 12
EXACT = 256
VMEM = 58 * 1024 * 1024
PARTS = ("z", "xl", "core", "y", "xh")
PLANE = ("xl", "y", "xh")
SHIFTS = (63, 32, 16, 8, 4, 2, 1)
LARGEST = 32767.0
TAIL = 16


def column_of(row):
    count = row.shape[1]
    across = lax.broadcasted_iota(jnp.int32, (count, count), 0)
    down = lax.broadcasted_iota(jnp.int32, (count, count), 1)
    return jnp.sum(jnp.where(across == down, row, 0.0), axis=1, keepdims=True)


def row_of(column):
    count = column.shape[0]
    across = lax.broadcasted_iota(jnp.int32, (count, count), 0)
    down = lax.broadcasted_iota(jnp.int32, (count, count), 1)
    return jnp.sum(jnp.where(across == down, column, 0.0), axis=0, keepdims=True)


def scaled(values):
    top = jnp.max(jnp.abs(values), axis=1, keepdims=True)
    scale, power = jnp.ones_like(top), jnp.zeros_like(top)
    for shift in SHIFTS:
        fits = top * 2.0**shift <= LARGEST
        factor = jnp.where(fits, 2.0**shift, 1.0)
        top, scale = top * factor, scale * factor
        power += jnp.where(fits, float(shift), 0.0)
    return jnp.round(values * scale).astype(jnp.int32).astype(jnp.int16), power


def undone(power):
    factor = jnp.ones_like(power)
    for shift in SHIFTS:
        has = power >= shift
        factor = factor * jnp.where(has, 2.0**-shift, 1.0)
        power = power - jnp.where(has, float(shift), 0.0)
    return factor


def prepare_kernel(
    features_ref,
    grad_ref,
    weight_ref,
    degree_ref,
    index_ref,
    edges_ref,
    old_index_ref,
    old_edges_ref,
    sent_ref,
    slots_ref,
):
    nodes, width = grad_ref.shape
    for at, (index, edges) in enumerate(
        ((index_ref, edges_ref), (old_index_ref, old_edges_ref))
    ):
        fields, _, slots = index.shape
        numbers = jnp.concatenate([edges[...]] + [index[field] for field in range(fields)], axis=0)
        numbers = jnp.concatenate(
            [numbers, jnp.zeros((TILE - HALF - fields, slots), jnp.int32)], axis=0
        )
        numbers = jnp.concatenate(
            [numbers, jnp.zeros((TILE, TILE - slots), jnp.int32)], axis=1
        )
        slots_ref[at, :slots, :] = numbers.astype(jnp.float32).T[:slots].astype(jnp.int32)
        slots_ref[at, slots:, :] = numbers[HALF : HALF + 8, :]

    product = lax.dot_general(
        grad_ref[...],
        weight_ref[...],
        (((1,), (1,)), ((), ())),
        preferred_element_type=jnp.float32,
    )
    degree = column_of(degree_ref[...].astype(jnp.float32))
    mean_grad = (product / degree).astype(jnp.bfloat16).astype(jnp.float32)
    values, grad_power = scaled(mean_grad)
    sent_ref[:nodes, :] = values
    values, feature_power = scaled(features_ref[...].astype(jnp.float32))
    sent_ref[nodes : 2 * nodes, :] = values
    lines = lax.broadcasted_iota(jnp.int32, (TAIL, nodes), 0)
    tail = jnp.where(lines == 0, row_of(grad_power), 0.0)
    tail = jnp.where(lines == 1, row_of(feature_power), tail)
    tail = jnp.concatenate([tail, jnp.zeros((TAIL, width - nodes), jnp.float32)], axis=1)
    sent_ref[2 * nodes :, :] = tail.astype(jnp.int32).astype(jnp.int16)


def prepare(features, old_grad, w_neigh, old_degree, tables):
    nodes, width = features.shape
    slots = tables[0].shape[-1]
    args = (features, old_grad, w_neigh, old_degree, *tables)
    outs = (
        jax.ShapeDtypeStruct((2 * nodes + TAIL, width), jnp.int16),
        jax.ShapeDtypeStruct((2, slots + 8, TILE), jnp.int32),
    )

    def whole(arg):
        return pl.BlockSpec(arg.shape, lambda _: (0,) * len(arg.shape))

    return pl.pallas_call(
        prepare_kernel,
        out_shape=outs,
        grid=(1,),
        in_specs=[whole(arg) for arg in args],
        out_specs=tuple(whole(out) for out in outs),
        compiler_params=pltpu.CompilerParams(vmem_limit_bytes=VMEM),
    )(*args)


def sums_kernel(
    lane_ref,
    new_own_info,
    new_other_info,
    old_own_info,
    old_other_info,
    own_ref,
    other_ref,
    sent_ref,
    out_ref,
    dst_rows,
    src_rows,
    counts,
    raw,
    tails,
    factors,
    held,
    total,
    wide,
    sems,
):
    lane = lane_ref[0]
    devices, nodes = out_ref.shape[0] // 2, out_ref.shape[2]
    senders = tails.shape[0]
    planes = senders // 2
    slots = own_ref.shape[1] - 8
    pairs = slots // 2
    infos = ((old_own_info, old_other_info), (new_own_info, new_other_info))

    tail_fetch = pltpu.make_async_copy(
        sent_ref.at[:, pl.ds(2 * nodes, TAIL), pl.ds(0, TILE)], tails, sems.at[2 * senders]
    )
    fetches = [
        [
            pltpu.make_async_copy(
                sent_ref.at[sender, pl.ds(array * nodes, nodes)],
                raw.at[array, pl.ds(sender * nodes, nodes)],
                sems.at[array * senders + sender],
            )
            for sender in range(senders)
        ]
        for array in range(2)
    ]
    tail_fetch.start()
    for copy in fetches[0] + fetches[1]:
        copy.start()

    def hold(array):
        powers = [tails[sender, array : array + 1, :] for sender in range(senders)]
        powers = jnp.concatenate(powers, axis=0).astype(jnp.int32).astype(jnp.float32)
        rest = jnp.ones((TILE - senders, TILE), jnp.float32)
        factor = jnp.concatenate([undone(powers), rest], axis=0).T
        for sender in range(senders):
            factors[sender * nodes : (sender + 1) * nodes] = jnp.broadcast_to(
                factor[:nodes, sender : sender + 1], (nodes, TILE)
            )

        def move(begin, into, size):
            rows = pl.ds(pl.multiple_of(begin, HALF), size)
            values = raw[array, rows, :].astype(jnp.int32).astype(jnp.float32)
            times = factors[rows, :]
            times = jnp.concatenate([times] * (values.shape[1] // TILE), axis=1)
            rows = pl.ds(pl.multiple_of(into, HALF), size)
            held[rows, :] = (values * times).astype(jnp.bfloat16)

        def move_plane(plane, carry):
            begin = plane * 2 * nodes
            move(begin + lane * HALF, plane * TILE, TILE)
            move(begin + (1 - lane) * TILE, planes * TILE + plane * HALF, HALF)
            return carry

        lax.fori_loop(0, planes, move_plane, 0)

    lanes = lax.broadcasted_iota(jnp.int32, (pairs, TILE), 1)
    left = lanes < HALF

    def plan(at, edges):
        even, odd = edges[pl.ds(0, pairs, 2), :], edges[pl.ds(1, pairs, 2), :]

        def field(at):
            return jnp.where(left, even[:, at : at + 1], odd[:, at : at + 1])

        values = jnp.where(left, even, pltpu.roll(odd, HALF, 1))
        column, count = field(HALF + 1), field(HALF + 2)
        plane = (column * 43) >> 7
        part = column - 3 * plane
        source = values & (TILE - 1)
        whole = part == 2 * lane
        own = whole | ((part == 1) & ((source >> 6) == lane))
        own &= (lanes & (HALF - 1)) < count
        place = jnp.where(whole, source, (source & (HALF - 1)) + (plane & 1) * HALF)
        place += jnp.where(left, 0, TILE)
        dst_rows[at] = jnp.where(own, values >> 7, -1).astype(jnp.float32)
        src_rows[at] = jnp.where(own, place, -1).astype(jnp.float32)
        return jnp.sum((even[:, HALF + 2 : HALF + 3] > 0).astype(jnp.int32))

    dst_ids = lax.broadcasted_iota(jnp.int32, (TILE, TILE), 0).astype(jnp.bfloat16)
    src_ids = lax.broadcasted_iota(jnp.int32, (2 * TILE, TILE), 0).astype(jnp.bfloat16)
    zero, unit = jnp.bfloat16(0), jnp.bfloat16(1)

    def spot(info, slot):
        row, column = info[0, slot], info[1, slot]
        plane = (column * 43) >> 7
        block = jnp.where(column - 3 * plane == 2 * lane, plane, planes + (plane >> 1))
        return block, pl.ds(pl.multiple_of(row * TILE, TILE), TILE)

    def pair_counts(at, pair):
        dst = dst_rows[at, pl.ds(pair, 1), :].astype(jnp.bfloat16)
        src = src_rows[at, pl.ds(pair, 1), :].astype(jnp.bfloat16)
        dst_hot = jnp.where(dst_ids == dst, unit, zero)
        src_hot = jnp.where(src_ids == src, unit, zero)
        return lax.dot_general(
            dst_hot, src_hot, (((1,), (1,)), ((), ())), preferred_element_type=jnp.float32
        ).astype(jnp.bfloat16)

    def build(at, info, first, last, unroll):
        counts[at] = jnp.zeros(counts.shape[1:], jnp.bfloat16)

        def add(turn, peak):
            found = [first + turn * unroll + pair for pair in range(unroll)]
            added = [pair_counts(at, pair) for pair in found]
            for pair, both in zip(found, added):
                for side in range(2):
                    block, rows = spot(info, 2 * pair + side)
                    sums = counts[at, block, rows, :]
                    sums = sums + both[:, side * TILE : (side + 1) * TILE]
                    counts[at, block, rows, :] = sums
                    peak = jnp.maximum(peak, sums)
            return peak

        start = jnp.zeros((TILE, TILE), jnp.bfloat16)
        return lax.fori_loop(0, pl.cdiv(last - first, unroll), add, start)

    def product(at):
        left_side = jnp.concatenate([counts[at, block] for block in range(counts.shape[1])], axis=1)
        return jnp.dot(left_side, held[...], preferred_element_type=jnp.float32)

    def put(array, half):
        where = half + lane - 2 * half * lane
        at = 2 * array + half
        return [
            pltpu.make_async_copy(
                total.at[at, pl.ds(device * nodes, nodes)],
                out_ref.at[where * devices + device, array],
                sems.at[2 * senders + 1 + at * devices + device],
            )
            for device in range(devices)
        ]

    peaks = []
    for array in range(2):
        for half, edges in enumerate((own_ref, other_ref)):
            at = 2 * array + half
            live_pairs = plan(at, edges.at[1 - array])
            peaks.append(build(at, infos[array][half], 0, live_pairs, UNROLL))
    tail_fetch.wait()
    for array in range(2):
        for copy in fetches[array]:
            copy.wait()
        hold(array)
        for half in range(2):
            at = 2 * array + half
            peak = jnp.max(peaks[at].astype(jnp.float32))

            @pl.when(peak < EXACT)
            def _(at=at):
                total[at] = product(at).astype(jnp.bfloat16)

            @pl.when(peak >= EXACT)
            def _(at=at, info=infos[array][half]):
                wide[...] = jnp.zeros_like(wide)

                def some(turn, carry):
                    build(at, info, 2 * turn, 2 * turn + 2, 2)
                    wide[...] += product(at)
                    return carry

                lax.fori_loop(0, pairs // 2, some, 0)
                total[at] = wide[...].astype(jnp.bfloat16)

            for copy in put(array, half):
                copy.start()
    for array in range(2):
        for half in range(2):
            for copy in put(array, half):
                copy.wait()


def edge_sums(lane, own, other, sent, devices, nodes):
    slots = own.shape[1] - 8
    senders, _, width = sent.shape
    depth, rows = senders * nodes, devices * nodes
    table = pl.BlockSpec(own.shape, lambda _, lane: (0, 0, 0))

    def info(graph):
        return pl.BlockSpec(
            (None, 8, TILE), lambda _, lane: (graph, slots // 8, 0), memory_space=pltpu.SMEM
        )

    far = pl.BlockSpec(memory_space=pl.ANY)
    return pl.pallas_call(
        sums_kernel,
        out_shape=jax.ShapeDtypeStruct((2 * devices, 2, nodes, width), jnp.bfloat16),
        grid_spec=pltpu.PrefetchScalarGridSpec(
            num_scalar_prefetch=1,
            grid=(1,),
            in_specs=[info(0), info(0), info(1), info(1), table, table, far],
            out_specs=far,
            scratch_shapes=[
                pltpu.VMEM((4, slots // 2, TILE), jnp.float32),
                pltpu.VMEM((4, slots // 2, TILE), jnp.float32),
                pltpu.VMEM((4, depth // TILE, rows, TILE), jnp.bfloat16),
                pltpu.VMEM((2, depth, width), jnp.int16),
                pltpu.VMEM((senders, TAIL, TILE), jnp.int16),
                pltpu.VMEM((depth, TILE), jnp.float32),
                pltpu.VMEM((depth, width), jnp.bfloat16),
                pltpu.VMEM((4, rows, width), jnp.bfloat16),
                pltpu.VMEM((rows, width), jnp.float32),
                pltpu.SemaphoreType.DMA((2 * senders + 1 + 4 * devices,)),
            ],
        ),
        compiler_params=pltpu.CompilerParams(vmem_limit_bytes=VMEM),
        cost_estimate=pl.CostEstimate(
            flops=16 * 10**9, bytes_accessed=20 * 10**6, transcendentals=0
        ),
    )(lane, own, other, own, other, own, other, sent)


def finish_kernel(
    parts_ref,
    features_ref,
    grad_ref,
    self_ref,
    neigh_ref,
    bias_ref,
    degree_ref,
    out_ref,
    grad_out_ref,
    parts,
    sems,
):
    senders = parts.shape[0]
    fetches = [
        pltpu.make_async_copy(parts_ref.at[sender], parts.at[sender], sems.at[sender])
        for sender in range(senders)
    ]
    for copy in fetches:
        copy.start()
    own_grad = lax.dot_general(
        grad_ref[...], self_ref[...], (((1,), (1,)), ((), ())), preferred_element_type=jnp.float32
    )
    own_out = jnp.dot(features_ref[...], self_ref[...], preferred_element_type=jnp.float32)
    degree = column_of(degree_ref[...].astype(jnp.float32))
    for copy in fetches:
        copy.wait()

    def summed(array):
        sums = parts[0, array].astype(jnp.float32)
        for sender in range(1, senders):
            sums += parts[sender, array].astype(jnp.float32)
        return sums

    mean = (summed(1) / degree).astype(jnp.bfloat16)
    grad_out_ref[...] = (own_grad + summed(0)).astype(jnp.bfloat16)
    preact = jnp.dot(mean, neigh_ref[...], preferred_element_type=jnp.float32)
    preact = own_out + preact + bias_ref[...]
    out_ref[...] = jnp.maximum(preact, 0.0).astype(jnp.bfloat16)


def finish(parts, features, old_grad, w_self, w_neigh, bias_term, degree):
    args = (features, old_grad, w_self, w_neigh, bias_term, degree)
    out = jax.ShapeDtypeStruct(features.shape, jnp.bfloat16)

    def whole(arg):
        return pl.BlockSpec(arg.shape, lambda _: (0,) * len(arg.shape))

    return pl.pallas_call(
        finish_kernel,
        out_shape=(out, out),
        grid=(1,),
        in_specs=[pl.BlockSpec(memory_space=pl.ANY)] + [whole(arg) for arg in args],
        out_specs=(whole(out), whole(out)),
        scratch_shapes=[
            pltpu.VMEM(parts.shape, jnp.bfloat16),
            pltpu.SemaphoreType.DMA((parts.shape[0],)),
        ],
        compiler_params=pltpu.CompilerParams(vmem_limit_bytes=VMEM),
    )(parts, *args)


def shards(
    features,
    degree,
    w_self,
    w_neigh,
    bias_term,
    tile_index,
    tile_edges,
    old_grad,
    old_degree,
    old_index,
    old_edges,
):
    nodes, width = features.shape
    devices = lax.axis_size("y") * lax.axis_size("xh")
    lane = lax.axis_index("xl")

    tables = []
    for index, edges in ((tile_index, tile_edges), (old_index, old_edges)):
        tables.append(jnp.transpose(index[0], (2, 0, 1)))
        tables.append(edges[0, 0].T)
    sent, own = prepare(features, old_grad, w_neigh, old_degree[None], tables)
    other = lax.ppermute(own, "xl", [(0, 1), (1, 0)])

    got = lax.all_gather(sent, ("z", "core"), axis=0, tiled=False)

    partial = edge_sums(lane.reshape(1), own, other, got, devices, nodes)
    parts = lax.all_to_all(partial, PLANE, 0, 0)
    return finish(parts, features, old_grad, w_self, w_neigh, bias_term[None], degree[None])


def solution(mesh):
    parts = Mesh(mesh.devices.reshape(16, 2, 2, 4, 2), PARTS)
    block = ("z", "xl", "core")
    side = ("y", "xh")
    in_specs = (
        P(PARTS, None),
        P(PARTS),
        P(),
        P(),
        P(),
        P(block, side, None, None),
        P(block, side, None, None),
        P(PARTS, None),
        P(PARTS),
        P(block, side, None, None),
        P(block, side, None, None),
    )
    out_specs = (P(PARTS, None), P(PARTS, None))
    return jax.shard_map(
        shards, mesh=parts, in_specs=in_specs, out_specs=out_specs, check_vma=False
    )
```

```python
import jax
import jax.numpy as jnp
from jax import lax
from jax.experimental import pallas as pl
from jax.experimental.pallas import tpu as pltpu
from jax.sharding import Mesh
from jax.sharding import PartitionSpec as P

TILE = 128
HALF = TILE // 2
UNROLL = 12
EXACT = 256
VMEM = 58 * 1024 * 1024
PARTS = ("z", "xl", "core", "y", "xh")
PLANE = ("xl", "y", "xh")
SHIFTS = (63, 32, 16, 8, 4, 2, 1)
LARGEST = 32767.0
TAIL = 8


def column_of(row):
    count = row.shape[1]
    across = lax.broadcasted_iota(jnp.int32, (count, count), 0)
    down = lax.broadcasted_iota(jnp.int32, (count, count), 1)
    return jnp.sum(jnp.where(across == down, row, 0.0), axis=1, keepdims=True)


def row_of(column):
    count = column.shape[0]
    across = lax.broadcasted_iota(jnp.int32, (count, count), 0)
    down = lax.broadcasted_iota(jnp.int32, (count, count), 1)
    return jnp.sum(jnp.where(across == down, column, 0.0), axis=0, keepdims=True)


def scaled(values):
    top = jnp.max(jnp.abs(values), axis=1, keepdims=True)
    scale, power = jnp.ones_like(top), jnp.zeros_like(top)
    for shift in SHIFTS:
        fits = top * 2.0**shift <= LARGEST
        factor = jnp.where(fits, 2.0**shift, 1.0)
        top, scale = top * factor, scale * factor
        power += jnp.where(fits, float(shift), 0.0)
    return jnp.round(values * scale).astype(jnp.int32).astype(jnp.int16), power


def undone(power):
    factor = jnp.ones_like(power)
    for shift in SHIFTS:
        has = power >= shift
        factor = factor * jnp.where(has, 2.0**-shift, 1.0)
        power = power - jnp.where(has, float(shift), 0.0)
    return factor


def prepare_kernel(
    features_ref,
    grad_ref,
    weight_ref,
    degree_ref,
    index_ref,
    edges_ref,
    old_index_ref,
    old_edges_ref,
    sent_ref,
    slots_ref,
):
    nodes, width = grad_ref.shape
    for at, (index, edges) in enumerate(
        ((index_ref, edges_ref), (old_index_ref, old_edges_ref))
    ):
        fields, _, slots = index.shape
        numbers = jnp.concatenate([edges[...]] + [index[field] for field in range(fields)], axis=0)
        numbers = jnp.concatenate(
            [numbers, jnp.zeros((TILE - HALF - fields, slots), jnp.int32)], axis=0
        )
        numbers = jnp.concatenate(
            [numbers, jnp.zeros((TILE, TILE - slots), jnp.int32)], axis=1
        )
        slots_ref[at, :slots, :] = numbers.astype(jnp.float32).T[:slots].astype(jnp.int32)
        slots_ref[at, slots:, :] = numbers[HALF : HALF + 8, :]

    product = lax.dot_general(
        grad_ref[...],
        weight_ref[...],
        (((1,), (1,)), ((), ())),
        preferred_element_type=jnp.float32,
    )
    degree = column_of(degree_ref[...].astype(jnp.float32))
    mean_grad = (product / degree).astype(jnp.bfloat16).astype(jnp.float32)
    values, grad_power = scaled(mean_grad)
    sent_ref[:nodes, :] = values
    values, feature_power = scaled(features_ref[...].astype(jnp.float32))
    sent_ref[nodes : 2 * nodes, :] = values
    lines = lax.broadcasted_iota(jnp.int32, (TAIL, nodes), 0)
    tail = jnp.where(lines == 0, row_of(grad_power), 0.0)
    tail = jnp.where(lines == 1, row_of(feature_power), tail)
    tail = jnp.concatenate([tail, jnp.zeros((TAIL, width - nodes), jnp.float32)], axis=1)
    sent_ref[2 * nodes :, :] = tail.astype(jnp.int32).astype(jnp.int16)


def prepare(features, old_grad, w_neigh, old_degree, tables):
    nodes, width = features.shape
    slots = tables[0].shape[-1]
    args = (features, old_grad, w_neigh, old_degree, *tables)
    outs = (
        jax.ShapeDtypeStruct((2 * nodes + TAIL, width), jnp.int16),
        jax.ShapeDtypeStruct((2, slots + 8, TILE), jnp.int32),
    )

    def whole(arg):
        return pl.BlockSpec(arg.shape, lambda _: (0,) * len(arg.shape))

    return pl.pallas_call(
        prepare_kernel,
        out_shape=outs,
        grid=(1,),
        in_specs=[whole(arg) for arg in args],
        out_specs=tuple(whole(out) for out in outs),
        compiler_params=pltpu.CompilerParams(vmem_limit_bytes=VMEM),
    )(*args)


def sums_kernel(
    lane_ref,
    new_own_info,
    new_other_info,
    old_own_info,
    old_other_info,
    own_ref,
    other_ref,
    sent_ref,
    out_ref,
    dst_rows,
    src_rows,
    counts,
    raw,
    factors,
    held,
    total,
    wide,
    sems,
):
    lane = lane_ref[0]
    devices, nodes = out_ref.shape[0] // 2, out_ref.shape[2]
    senders = raw.shape[0]
    planes = senders // 2
    slots = own_ref.shape[1] - 8
    pairs = slots // 2
    infos = ((old_own_info, old_other_info), (new_own_info, new_other_info))

    fetches = [
        pltpu.make_async_copy(sent_ref.at[sender], raw.at[sender], sems.at[sender])
        for sender in range(senders)
    ]
    for copy in fetches:
        copy.start()

    def hold(array):
        first = array * nodes
        powers = [raw[sender, 2 * nodes :, :TILE][array : array + 1] for sender in range(senders)]
        powers = [power.astype(jnp.int32).astype(jnp.float32) for power in powers]
        rest = jnp.ones((TILE - senders, TILE), jnp.float32)
        factor = jnp.concatenate([undone(jnp.concatenate(powers, axis=0)), rest], axis=0).T
        for sender in range(senders):
            factors[sender] = jnp.broadcast_to(
                factor[:nodes, sender : sender + 1], (nodes, TILE)
            )

        def move(sender, begin, into, size):
            values = raw[sender, first + begin : first + begin + size, :]
            values = values.astype(jnp.int32).astype(jnp.float32)
            times = factors[sender, begin : begin + size, :]
            times = jnp.concatenate([times] * (values.shape[1] // TILE), axis=1)
            rows = pl.ds(pl.multiple_of(into, 16), size)
            held[rows, :] = (values * times).astype(jnp.bfloat16)

        def move_plane(plane, carry):
            whole, part = plane * TILE, planes * TILE + plane * HALF
            one, two = 2 * plane, 2 * plane + 1

            @pl.when(lane == 0)
            def _():
                move(one, 0, whole, nodes)
                move(two, 0, whole + nodes, TILE - nodes)
                move(two, TILE - nodes, part, HALF)

            @pl.when(lane == 1)
            def _():
                move(one, 0, part, HALF)
                move(one, HALF, whole, nodes - HALF)
                move(two, 0, whole + nodes - HALF, nodes)

            return carry

        lax.fori_loop(0, planes, move_plane, 0)

    lanes = lax.broadcasted_iota(jnp.int32, (pairs, TILE), 1)
    left = lanes < HALF

    def plan(at, edges):
        even, odd = edges[pl.ds(0, pairs, 2), :], edges[pl.ds(1, pairs, 2), :]

        def field(at):
            return jnp.where(left, even[:, at : at + 1], odd[:, at : at + 1])

        values = jnp.where(left, even, pltpu.roll(odd, HALF, 1))
        column, count = field(HALF + 1), field(HALF + 2)
        plane = (column * 43) >> 7
        part = column - 3 * plane
        source = values & (TILE - 1)
        whole = part == 2 * lane
        own = whole | ((part == 1) & ((source >> 6) == lane))
        own &= (lanes & (HALF - 1)) < count
        place = jnp.where(whole, source, (source & (HALF - 1)) + (plane & 1) * HALF)
        place += jnp.where(left, 0, TILE)
        dst_rows[at] = jnp.where(own, values >> 7, -1).astype(jnp.float32)
        src_rows[at] = jnp.where(own, place, -1).astype(jnp.float32)
        return jnp.sum((even[:, HALF + 2 : HALF + 3] > 0).astype(jnp.int32))

    dst_ids = lax.broadcasted_iota(jnp.int32, (TILE, TILE), 0).astype(jnp.bfloat16)
    src_ids = lax.broadcasted_iota(jnp.int32, (2 * TILE, TILE), 0).astype(jnp.bfloat16)
    zero, unit = jnp.bfloat16(0), jnp.bfloat16(1)

    def spot(info, slot):
        row, column = info[0, slot], info[1, slot]
        plane = (column * 43) >> 7
        block = jnp.where(column - 3 * plane == 2 * lane, plane, planes + (plane >> 1))
        return block, pl.ds(pl.multiple_of(row * TILE, TILE), TILE)

    def pair_counts(at, pair):
        dst = dst_rows[at, pl.ds(pair, 1), :].astype(jnp.bfloat16)
        src = src_rows[at, pl.ds(pair, 1), :].astype(jnp.bfloat16)
        dst_hot = jnp.where(dst_ids == dst, unit, zero)
        src_hot = jnp.where(src_ids == src, unit, zero)
        return lax.dot_general(
            dst_hot, src_hot, (((1,), (1,)), ((), ())), preferred_element_type=jnp.float32
        ).astype(jnp.bfloat16)

    def clear(at):
        counts[at] = jnp.zeros(counts.shape[1:], jnp.bfloat16)

    def build(at, info, first, last, unroll):
        def add(turn, peak):
            found = [first + turn * unroll + pair for pair in range(unroll)]
            added = [pair_counts(at, pair) for pair in found]
            for pair, both in zip(found, added):
                for side in range(2):
                    block, rows = spot(info, 2 * pair + side)
                    sums = counts[at, block, rows, :]
                    sums = sums + both[:, side * TILE : (side + 1) * TILE]
                    counts[at, block, rows, :] = sums
                    peak = jnp.maximum(peak, sums)
            return peak

        start = jnp.zeros((TILE, TILE), jnp.bfloat16)
        return lax.fori_loop(0, pl.cdiv(last - first, unroll), add, start)

    def product(at):
        left_side = jnp.concatenate([counts[at, block] for block in range(counts.shape[1])], axis=1)
        return jnp.dot(left_side, held[...], preferred_element_type=jnp.float32)

    def put(array, half):
        where = half + lane - 2 * half * lane
        at = 2 * array + half
        return [
            pltpu.make_async_copy(
                total.at[at, pl.ds(device * nodes, nodes)],
                out_ref.at[where * devices + device, array],
                sems.at[senders + at * devices + device],
            )
            for device in range(devices)
        ]

    for half in range(2):
        clear(half)
    for array in range(2):
        top = jnp.zeros((TILE, TILE), jnp.bfloat16)
        for half, edges in enumerate((own_ref, other_ref)):
            at = 2 * array + half
            live_pairs = plan(at, edges.at[1 - array])
            top = jnp.maximum(top, build(at, infos[array][half], 0, live_pairs, UNROLL))
        top = jnp.max(top.astype(jnp.float32))
        if array == 0:
            for copy in fetches:
                copy.wait()
        hold(array)

        @pl.when(top < EXACT)
        def _(array=array):
            for half in range(2):
                at = 2 * array + half
                total[at] = product(at).astype(jnp.bfloat16)
                if array == 0:
                    clear(2 + half)
                for copy in put(array, half):
                    copy.start()

        @pl.when(top >= EXACT)
        def _(array=array):
            for half in range(2):
                at, info = 2 * array + half, infos[array][half]
                wide[...] = jnp.zeros_like(wide)

                def some(turn, carry, at=at, info=info):
                    clear(at)
                    build(at, info, 2 * turn, 2 * turn + 2, 2)
                    wide[...] += product(at)
                    return carry

                lax.fori_loop(0, pairs // 2, some, 0)
                total[at] = wide[...].astype(jnp.bfloat16)
                if array == 0:
                    clear(2 + half)
                for copy in put(array, half):
                    copy.start()

    for array in range(2):
        for half in range(2):
            for copy in put(array, half):
                copy.wait()


def edge_sums(lane, own, other, sent, devices, nodes):
    slots = own.shape[1] - 8
    senders, _, width = sent.shape
    depth, rows = senders * nodes, devices * nodes
    table = pl.BlockSpec(own.shape, lambda _, lane: (0, 0, 0))

    def info(graph):
        return pl.BlockSpec(
            (None, 8, TILE), lambda _, lane: (graph, slots // 8, 0), memory_space=pltpu.SMEM
        )

    far = pl.BlockSpec(memory_space=pl.ANY)
    return pl.pallas_call(
        sums_kernel,
        out_shape=jax.ShapeDtypeStruct((2 * devices, 2, nodes, width), jnp.bfloat16),
        grid_spec=pltpu.PrefetchScalarGridSpec(
            num_scalar_prefetch=1,
            grid=(1,),
            in_specs=[info(0), info(0), info(1), info(1), table, table, far],
            out_specs=far,
            scratch_shapes=[
                pltpu.VMEM((4, slots // 2, TILE), jnp.float32),
                pltpu.VMEM((4, slots // 2, TILE), jnp.float32),
                pltpu.VMEM((4, depth // TILE, rows, TILE), jnp.bfloat16),
                pltpu.VMEM(sent.shape, jnp.int16),
                pltpu.VMEM((senders, nodes, TILE), jnp.float32),
                pltpu.VMEM((depth, width), jnp.bfloat16),
                pltpu.VMEM((4, rows, width), jnp.bfloat16),
                pltpu.VMEM((rows, width), jnp.float32),
                pltpu.SemaphoreType.DMA((senders + 4 * devices,)),
            ],
        ),
        compiler_params=pltpu.CompilerParams(vmem_limit_bytes=VMEM),
        cost_estimate=pl.CostEstimate(
            flops=16 * 10**9, bytes_accessed=20 * 10**6, transcendentals=0
        ),
    )(lane, own, other, own, other, own, other, sent)


def finish_kernel(
    parts_ref,
    features_ref,
    grad_ref,
    self_ref,
    neigh_ref,
    bias_ref,
    degree_ref,
    out_ref,
    grad_out_ref,
    parts,
    features,
    grad,
    w_self,
    w_neigh,
    own_out,
    own_grad,
    mean,
    sems,
):
    senders = parts.shape[0]
    sources = (features_ref, grad_ref, self_ref, neigh_ref)
    ends = (features, grad, w_self, w_neigh)
    fetches = [
        pltpu.make_async_copy(source, end, sems.at[at])
        for at, (source, end) in enumerate(zip(sources, ends))
    ]
    part_fetches = [
        pltpu.make_async_copy(parts_ref.at[at], parts.at[at], sems.at[len(ends) + at])
        for at in range(senders)
    ]
    for copy in fetches + part_fetches:
        copy.start()
    degree = column_of(degree_ref[...].astype(jnp.float32))
    for copy in fetches:
        copy.wait()
    own_grad[...] = lax.dot_general(
        grad[...], w_self[...], (((1,), (1,)), ((), ())), preferred_element_type=jnp.float32
    )
    own_out[...] = jnp.dot(features[...], w_self[...], preferred_element_type=jnp.float32)
    for copy in part_fetches:
        copy.wait()
    for begin in range(0, features.shape[0], 16):
        rows = pl.ds(begin, 16)

        def summed(array):
            return sum(parts[at, array, rows, :].astype(jnp.float32) for at in range(senders))

        mean[rows, :] = (summed(1) / degree[begin : begin + 16]).astype(jnp.bfloat16)
        grad_out_ref[rows, :] = (own_grad[rows, :] + summed(0)).astype(jnp.bfloat16)
    preact = jnp.dot(mean[...], w_neigh[...], preferred_element_type=jnp.float32)
    preact = own_out[...] + preact + bias_ref[...]
    out_ref[...] = jnp.maximum(preact, 0.0).astype(jnp.bfloat16)


def finish(parts, features, old_grad, w_self, w_neigh, bias_term, degree):
    out = jax.ShapeDtypeStruct(features.shape, jnp.bfloat16)
    far = pl.BlockSpec(memory_space=pl.ANY)

    def whole(arg):
        return pl.BlockSpec(arg.shape, lambda _: (0,) * len(arg.shape))

    held = (parts, features, old_grad, w_self, w_neigh)
    return pl.pallas_call(
        finish_kernel,
        out_shape=(out, out),
        grid=(1,),
        in_specs=[far] * 5 + [whole(bias_term), whole(degree)],
        out_specs=(whole(out), whole(out)),
        scratch_shapes=[pltpu.VMEM(arg.shape, jnp.bfloat16) for arg in held]
        + [pltpu.VMEM(features.shape, jnp.float32)] * 2
        + [
            pltpu.VMEM(features.shape, jnp.bfloat16),
            pltpu.SemaphoreType.DMA((4 + parts.shape[0],)),
        ],
        compiler_params=pltpu.CompilerParams(vmem_limit_bytes=VMEM),
    )(parts, features, old_grad, w_self, w_neigh, bias_term, degree)


def shards(
    features,
    degree,
    w_self,
    w_neigh,
    bias_term,
    tile_index,
    tile_edges,
    old_grad,
    old_degree,
    old_index,
    old_edges,
):
    nodes, width = features.shape
    devices = lax.axis_size("y") * lax.axis_size("xh")
    lane = lax.axis_index("xl")

    tables = []
    for index, edges in ((tile_index, tile_edges), (old_index, old_edges)):
        tables.append(jnp.transpose(index[0], (2, 0, 1)))
        tables.append(edges[0, 0].T)
    sent, own = prepare(features, old_grad, w_neigh, old_degree[None], tables)
    other = lax.ppermute(own, "xl", [(0, 1), (1, 0)])

    got = lax.all_gather(sent, ("z", "core"), axis=0, tiled=False)

    partial = edge_sums(lane.reshape(1), own, other, got, devices, nodes)
    parts = lax.all_to_all(partial, PLANE, 0, 0)
    return finish(parts, features, old_grad, w_self, w_neigh, bias_term[None], degree[None])


def solution(mesh):
    parts = Mesh(mesh.devices.reshape(16, 2, 2, 4, 2), PARTS)
    block = ("z", "xl", "core")
    side = ("y", "xh")
    in_specs = (
        P(PARTS, None),
        P(PARTS),
        P(),
        P(),
        P(),
        P(block, side, None, None),
        P(block, side, None, None),
        P(PARTS, None),
        P(PARTS),
        P(block, side, None, None),
        P(block, side, None, None),
    )
    out_specs = (P(PARTS, None), P(PARTS, None))
    return jax.shard_map(
        shards, mesh=parts, in_specs=in_specs, out_specs=out_specs, check_vma=False
    )
```

```python
import jax
import jax.numpy as jnp
from jax import lax
from jax.experimental import pallas as pl
from jax.experimental.pallas import tpu as pltpu
from jax.sharding import Mesh
from jax.sharding import PartitionSpec as P

TILE = 128
HALF = TILE // 2
UNROLL = 12
EXACT = 256
VMEM = 58 * 1024 * 1024
NEAR = 56 * 1024 * 1024
PARTS = ("z", "xl", "core", "y", "xh")
PLANE = ("xl", "y", "xh")
SHIFTS = (63, 32, 16, 8, 4, 2, 1)
LARGEST = 32767.0
TAIL = 8


def column_of(row):
    count = row.shape[1]
    across = lax.broadcasted_iota(jnp.int32, (count, count), 0)
    down = lax.broadcasted_iota(jnp.int32, (count, count), 1)
    return jnp.sum(jnp.where(across == down, row, 0.0), axis=1, keepdims=True)


def row_of(column):
    count = column.shape[0]
    across = lax.broadcasted_iota(jnp.int32, (count, count), 0)
    down = lax.broadcasted_iota(jnp.int32, (count, count), 1)
    return jnp.sum(jnp.where(across == down, column, 0.0), axis=0, keepdims=True)


def scaled(values):
    top = jnp.max(jnp.abs(values), axis=1, keepdims=True)
    scale, power = jnp.ones_like(top), jnp.zeros_like(top)
    for shift in SHIFTS:
        fits = top * 2.0**shift <= LARGEST
        factor = jnp.where(fits, 2.0**shift, 1.0)
        top, scale = top * factor, scale * factor
        power += jnp.where(fits, float(shift), 0.0)
    return jnp.round(values * scale).astype(jnp.int32).astype(jnp.int16), power


def undone(power):
    factor = jnp.ones_like(power)
    for shift in SHIFTS:
        has = power >= shift
        factor = factor * jnp.where(has, 2.0**-shift, 1.0)
        power = power - jnp.where(has, float(shift), 0.0)
    return factor


def prepare_kernel(
    features_ref,
    grad_ref,
    weight_ref,
    degree_ref,
    index_ref,
    edges_ref,
    old_index_ref,
    old_edges_ref,
    sent_ref,
    slots_ref,
):
    nodes, width = grad_ref.shape
    for at, (index, edges) in enumerate(
        ((index_ref, edges_ref), (old_index_ref, old_edges_ref))
    ):
        fields, _, slots = index.shape
        numbers = jnp.concatenate([edges[...]] + [index[field] for field in range(fields)], axis=0)
        numbers = jnp.concatenate(
            [numbers, jnp.zeros((TILE - HALF - fields, slots), jnp.int32)], axis=0
        )
        numbers = jnp.concatenate(
            [numbers, jnp.zeros((TILE, TILE - slots), jnp.int32)], axis=1
        )
        slots_ref[at, :slots, :] = numbers.astype(jnp.float32).T[:slots].astype(jnp.int32)
        slots_ref[at, slots:, :] = numbers[HALF : HALF + 8, :]

    product = lax.dot_general(
        grad_ref[...],
        weight_ref[...],
        (((1,), (1,)), ((), ())),
        preferred_element_type=jnp.float32,
    )
    degree = column_of(degree_ref[...].astype(jnp.float32))
    mean_grad = (product / degree).astype(jnp.bfloat16).astype(jnp.float32)
    values, grad_power = scaled(mean_grad)
    sent_ref[:nodes, :] = values
    values, feature_power = scaled(features_ref[...].astype(jnp.float32))
    sent_ref[nodes : 2 * nodes, :] = values
    lines = lax.broadcasted_iota(jnp.int32, (TAIL, nodes), 0)
    tail = jnp.where(lines == 0, row_of(grad_power), 0.0)
    tail = jnp.where(lines == 1, row_of(feature_power), tail)
    tail = jnp.concatenate([tail, jnp.zeros((TAIL, width - nodes), jnp.float32)], axis=1)
    sent_ref[2 * nodes :, :] = tail.astype(jnp.int32).astype(jnp.int16)


def prepare(features, old_grad, w_neigh, old_degree, tables):
    nodes, width = features.shape
    slots = tables[0].shape[-1]
    args = (features, old_grad, w_neigh, old_degree, *tables)
    outs = (
        jax.ShapeDtypeStruct((2 * nodes + TAIL, width), jnp.int16),
        jax.ShapeDtypeStruct((2, slots + 8, TILE), jnp.int32),
    )

    def whole(arg):
        return pl.BlockSpec(arg.shape, lambda _: (0,) * len(arg.shape))

    return pl.pallas_call(
        prepare_kernel,
        out_shape=outs,
        grid=(1,),
        in_specs=[whole(arg) for arg in args],
        out_specs=tuple(whole(out) for out in outs),
        compiler_params=pltpu.CompilerParams(vmem_limit_bytes=VMEM),
    )(*args)


def sums_kernel(
    lane_ref,
    own_ref,
    other_ref,
    sent_ref,
    out_ref,
    infos,
    dst_rows,
    src_rows,
    counts,
    raw,
    factors,
    held,
    wide,
    sems,
):
    lane = lane_ref[0]
    devices, nodes = out_ref.shape[0] // 2, out_ref.shape[2]
    senders = raw.shape[0]
    planes = senders // 2
    slots = own_ref.shape[1] - 8
    pairs = slots // 2
    info_fetches = [
        pltpu.make_async_copy(
            table.at[1 - array, pl.ds(slots, 8)],
            infos.at[2 * array + half],
            sems.at[2 * array + half],
        )
        for array in range(2)
        for half, table in enumerate((own_ref, other_ref))
    ]
    fetch = pltpu.make_async_copy(sent_ref, raw, sems.at[4])
    fetch.start()
    for copy in info_fetches:
        copy.start()

    def hold(array):
        first = array * nodes
        powers = [raw[sender, 2 * nodes :, :TILE][array : array + 1] for sender in range(senders)]
        powers = [power.astype(jnp.int32).astype(jnp.float32) for power in powers]
        rest = jnp.ones((TILE - senders, TILE), jnp.float32)
        factor = jnp.concatenate([undone(jnp.concatenate(powers, axis=0)), rest], axis=0).T
        for sender in range(senders):
            factors[sender] = jnp.broadcast_to(
                factor[:nodes, sender : sender + 1], (nodes, TILE)
            )

        def move(sender, begin, into, size):
            values = raw[sender, first + begin : first + begin + size, :]
            values = values.astype(jnp.int32).astype(jnp.float32)
            times = factors[sender, begin : begin + size, :]
            times = jnp.concatenate([times] * (values.shape[1] // TILE), axis=1)
            rows = pl.ds(pl.multiple_of(into, 16), size)
            held[rows, :] = (values * times).astype(jnp.bfloat16)

        def move_plane(plane, carry):
            whole, part = plane * TILE, planes * TILE + plane * HALF
            one, two = 2 * plane, 2 * plane + 1

            @pl.when(lane == 0)
            def _():
                move(one, 0, whole, nodes)
                move(two, 0, whole + nodes, TILE - nodes)
                move(two, TILE - nodes, part, HALF)

            @pl.when(lane == 1)
            def _():
                move(one, 0, part, HALF)
                move(one, HALF, whole, nodes - HALF)
                move(two, 0, whole + nodes - HALF, nodes)

            return carry

        lax.fori_loop(0, planes, move_plane, 0)

    lanes = lax.broadcasted_iota(jnp.int32, (pairs, TILE), 1)
    left = lanes < HALF

    def plan(at, edges):
        even, odd = edges[pl.ds(0, pairs, 2), :], edges[pl.ds(1, pairs, 2), :]

        def field(at):
            return jnp.where(left, even[:, at : at + 1], odd[:, at : at + 1])

        values = jnp.where(left, even, pltpu.roll(odd, HALF, 1))
        column, count = field(HALF + 1), field(HALF + 2)
        plane = (column * 43) >> 7
        part = column - 3 * plane
        source = values & (TILE - 1)
        whole = part == 2 * lane
        own = whole | ((part == 1) & ((source >> 6) == lane))
        own &= (lanes & (HALF - 1)) < count
        place = jnp.where(whole, source, (source & (HALF - 1)) + (plane & 1) * HALF)
        place += jnp.where(left, 0, TILE)
        dst_rows[at] = jnp.where(own, values >> 7, -1).astype(jnp.float32)
        src_rows[at] = jnp.where(own, place, -1).astype(jnp.float32)
        return jnp.sum((even[:, HALF + 2 : HALF + 3] > 0).astype(jnp.int32))

    dst_ids = lax.broadcasted_iota(jnp.int32, (TILE, TILE), 0).astype(jnp.bfloat16)
    src_ids = lax.broadcasted_iota(jnp.int32, (2 * TILE, TILE), 0).astype(jnp.bfloat16)
    zero, unit = jnp.bfloat16(0), jnp.bfloat16(1)

    def spot(at, slot):
        row, column = infos[at, 0, slot], infos[at, 1, slot]
        plane = (column * 43) >> 7
        block = jnp.where(column - 3 * plane == 2 * lane, plane, planes + (plane >> 1))
        return block, pl.ds(pl.multiple_of(row * TILE, TILE), TILE)

    def pair_counts(at, pair):
        dst = dst_rows[at, pl.ds(pair, 1), :].astype(jnp.bfloat16)
        src = src_rows[at, pl.ds(pair, 1), :].astype(jnp.bfloat16)
        dst_hot = jnp.where(dst_ids == dst, unit, zero)
        src_hot = jnp.where(src_ids == src, unit, zero)
        return lax.dot_general(
            dst_hot, src_hot, (((1,), (1,)), ((), ())), preferred_element_type=jnp.float32
        ).astype(jnp.bfloat16)

    def clear(at):
        counts[at] = jnp.zeros(counts.shape[1:], jnp.bfloat16)

    def build(at, first, last, unroll):
        def add(turn, peak):
            found = [first + turn * unroll + pair for pair in range(unroll)]
            added = [pair_counts(at, pair) for pair in found]
            for pair, both in zip(found, added):
                for side in range(2):
                    block, rows = spot(at, 2 * pair + side)
                    sums = counts[at, block, rows, :]
                    sums = sums + both[:, side * TILE : (side + 1) * TILE]
                    counts[at, block, rows, :] = sums
                    peak = jnp.maximum(peak, sums)
            return peak

        start = jnp.zeros((TILE, TILE), jnp.bfloat16)
        return lax.fori_loop(0, pl.cdiv(last - first, unroll), add, start)

    def product(at):
        left_side = jnp.concatenate([counts[at, block] for block in range(counts.shape[1])], axis=1)
        return jnp.dot(left_side, held[...], preferred_element_type=jnp.float32)

    def put(array, half, sums):
        where = half + lane - 2 * half * lane
        for device in range(devices):
            rows = sums[device * nodes : (device + 1) * nodes]
            out_ref[where * devices + device, array] = rows.astype(jnp.bfloat16)

    for half in range(2):
        clear(half)
    for copy in info_fetches:
        copy.wait()
    for array in range(2):
        top = jnp.zeros((TILE, TILE), jnp.bfloat16)
        for half, edges in enumerate((own_ref, other_ref)):
            at = 2 * array + half
            live_pairs = plan(at, edges.at[1 - array])
            top = jnp.maximum(top, build(at, 0, live_pairs, UNROLL))
        top = jnp.max(top.astype(jnp.float32))
        if array == 0:
            fetch.wait()
        hold(array)

        @pl.when(top < EXACT)
        def _(array=array):
            for half in range(2):
                put(array, half, product(2 * array + half))
                if array == 0:
                    clear(2 + half)

        @pl.when(top >= EXACT)
        def _(array=array):
            for half in range(2):
                at = 2 * array + half
                wide[...] = jnp.zeros_like(wide)

                def some(turn, carry, at=at):
                    clear(at)
                    build(at, 2 * turn, 2 * turn + 2, 2)
                    wide[...] += product(at)
                    return carry

                lax.fori_loop(0, pairs // 2, some, 0)
                put(array, half, wide[...])
                if array == 0:
                    clear(2 + half)


def edge_sums(lane, own, other, sent, devices, nodes):
    slots = own.shape[1] - 8
    senders, _, width = sent.shape
    depth, rows = senders * nodes, devices * nodes
    near = pl.BlockSpec(memory_space=pltpu.VMEM)
    return pl.pallas_call(
        sums_kernel,
        out_shape=jax.ShapeDtypeStruct((2 * devices, 2, nodes, width), jnp.bfloat16),
        in_specs=[pl.BlockSpec(memory_space=pltpu.SMEM), near, near, pl.BlockSpec(memory_space=pl.ANY)],
        out_specs=near,
        scratch_shapes=[
            pltpu.SMEM((4, 8, TILE), jnp.int32),
            pltpu.VMEM((4, slots // 2, TILE), jnp.float32),
            pltpu.VMEM((4, slots // 2, TILE), jnp.float32),
            pltpu.VMEM((4, depth // TILE, rows, TILE), jnp.bfloat16),
            pltpu.VMEM(sent.shape, jnp.int16),
            pltpu.VMEM((senders, nodes, TILE), jnp.float32),
            pltpu.VMEM((depth, width), jnp.bfloat16),
            pltpu.VMEM((rows, width), jnp.float32),
            pltpu.SemaphoreType.DMA((5,)),
        ],
        compiler_params=pltpu.CompilerParams(vmem_limit_bytes=NEAR),
        cost_estimate=pl.CostEstimate(
            flops=16 * 10**9, bytes_accessed=20 * 10**6, transcendentals=0
        ),
    )(lane, own, other, sent)


def finish_kernel(
    parts,
    features,
    grad,
    w_self,
    w_neigh,
    bias_ref,
    degree_ref,
    out_ref,
    grad_out_ref,
    own_grad,
    mean,
):
    senders = parts.shape[0]
    degree = column_of(degree_ref[...].astype(jnp.float32))
    own_grad[...] = lax.dot_general(
        grad[...], w_self[...], (((1,), (1,)), ((), ())), preferred_element_type=jnp.float32
    )
    for begin in range(0, features.shape[0], 16):
        rows = pl.ds(begin, 16)

        def summed(array):
            return sum(parts[at, array, rows, :].astype(jnp.float32) for at in range(senders))

        mean[rows, :] = (summed(1) / degree[begin : begin + 16]).astype(jnp.bfloat16)
        grad_out_ref[rows, :] = (own_grad[rows, :] + summed(0)).astype(jnp.bfloat16)
    preact = jnp.dot(features[...], w_self[...], preferred_element_type=jnp.float32)
    preact = preact + jnp.dot(mean[...], w_neigh[...], preferred_element_type=jnp.float32)
    out_ref[...] = jnp.maximum(preact + bias_ref[...], 0.0).astype(jnp.bfloat16)


def finish(parts, features, old_grad, w_self, w_neigh, bias_term, degree):
    out = jax.ShapeDtypeStruct(features.shape, jnp.bfloat16)
    return pl.pallas_call(
        finish_kernel,
        out_shape=(out, out),
        scratch_shapes=[
            pltpu.VMEM(features.shape, jnp.float32),
            pltpu.VMEM(features.shape, jnp.bfloat16),
        ],
        compiler_params=pltpu.CompilerParams(vmem_limit_bytes=16 * 1024 * 1024),
    )(parts, features, old_grad, w_self, w_neigh, bias_term, degree)


def shards(
    features,
    degree,
    w_self,
    w_neigh,
    bias_term,
    tile_index,
    tile_edges,
    old_grad,
    old_degree,
    old_index,
    old_edges,
):
    nodes, width = features.shape
    devices = lax.axis_size("y") * lax.axis_size("xh")
    lane = lax.axis_index("xl")

    tables = []
    for index, edges in ((tile_index, tile_edges), (old_index, old_edges)):
        tables.append(jnp.transpose(index[0], (2, 0, 1)))
        tables.append(edges[0, 0].T)
    sent, own = prepare(features, old_grad, w_neigh, old_degree[None], tables)
    other = lax.ppermute(own, "xl", [(0, 1), (1, 0)])

    got = lax.all_gather(sent, ("z", "core"), axis=0, tiled=False)

    partial = edge_sums(lane.reshape(1), own, other, got, devices, nodes)
    parts = lax.all_to_all(partial, PLANE, 0, 0)
    return finish(parts, features, old_grad, w_self, w_neigh, bias_term[None], degree[None])


def solution(mesh):
    parts = Mesh(mesh.devices.reshape(16, 2, 2, 4, 2), PARTS)
    block = ("z", "xl", "core")
    side = ("y", "xh")
    in_specs = (
        P(PARTS, None),
        P(PARTS),
        P(),
        P(),
        P(),
        P(block, side, None, None),
        P(block, side, None, None),
        P(PARTS, None),
        P(PARTS),
        P(block, side, None, None),
        P(block, side, None, None),
    )
    out_specs = (P(PARTS, None), P(PARTS, None))
    return jax.shard_map(
        shards, mesh=parts, in_specs=in_specs, out_specs=out_specs, check_vma=False
    )
```

```python
import jax
import jax.numpy as jnp
from jax import lax
from jax.experimental import pallas as pl
from jax.experimental.pallas import tpu as pltpu
from jax.sharding import Mesh
from jax.sharding import PartitionSpec as P

TILE = 128
HALF = TILE // 2
UNROLL = 12
EXACT = 256
VMEM = 58 * 1024 * 1024
NEAR = 52 * 1024 * 1024
PARTS = ("z", "xl", "core", "y", "xh")
PLANE = ("xl", "y", "xh")
SHIFTS = (63, 32, 16, 8, 4, 2, 1)
LARGEST = 32767.0
TAIL = 8


def column_of(row):
    count = row.shape[1]
    across = lax.broadcasted_iota(jnp.int32, (count, count), 0)
    down = lax.broadcasted_iota(jnp.int32, (count, count), 1)
    return jnp.sum(jnp.where(across == down, row, 0.0), axis=1, keepdims=True)


def row_of(column):
    count = column.shape[0]
    across = lax.broadcasted_iota(jnp.int32, (count, count), 0)
    down = lax.broadcasted_iota(jnp.int32, (count, count), 1)
    return jnp.sum(jnp.where(across == down, column, 0.0), axis=0, keepdims=True)


def scaled(values):
    top = jnp.max(jnp.abs(values), axis=1, keepdims=True)
    scale, power = jnp.ones_like(top), jnp.zeros_like(top)
    for shift in SHIFTS:
        fits = top * 2.0**shift <= LARGEST
        factor = jnp.where(fits, 2.0**shift, 1.0)
        top, scale = top * factor, scale * factor
        power += jnp.where(fits, float(shift), 0.0)
    return jnp.round(values * scale).astype(jnp.int32).astype(jnp.int16), power


def undone(power):
    factor = jnp.ones_like(power)
    for shift in SHIFTS:
        has = power >= shift
        factor = factor * jnp.where(has, 2.0**-shift, 1.0)
        power = power - jnp.where(has, float(shift), 0.0)
    return factor


def prepare_kernel(
    features_ref,
    grad_ref,
    weight_ref,
    degree_ref,
    index_ref,
    edges_ref,
    old_index_ref,
    old_edges_ref,
    sent_ref,
    slots_ref,
):
    nodes, width = grad_ref.shape
    for at, (index, edges) in enumerate(
        ((index_ref, edges_ref), (old_index_ref, old_edges_ref))
    ):
        fields, _, slots = index.shape
        numbers = jnp.concatenate([edges[...]] + [index[field] for field in range(fields)], axis=0)
        numbers = jnp.concatenate(
            [numbers, jnp.zeros((TILE - HALF - fields, slots), jnp.int32)], axis=0
        )
        numbers = jnp.concatenate(
            [numbers, jnp.zeros((TILE, TILE - slots), jnp.int32)], axis=1
        )
        slots_ref[at, :slots, :] = numbers.astype(jnp.float32).T[:slots].astype(jnp.int32)
        slots_ref[at, slots:, :] = numbers[HALF : HALF + 8, :]

    product = lax.dot_general(
        grad_ref[...],
        weight_ref[...],
        (((1,), (1,)), ((), ())),
        preferred_element_type=jnp.float32,
    )
    degree = column_of(degree_ref[...].astype(jnp.float32))
    mean_grad = (product / degree).astype(jnp.bfloat16).astype(jnp.float32)
    values, grad_power = scaled(mean_grad)
    sent_ref[:nodes, :] = values
    values, feature_power = scaled(features_ref[...].astype(jnp.float32))
    sent_ref[nodes : 2 * nodes, :] = values
    lines = lax.broadcasted_iota(jnp.int32, (TAIL, nodes), 0)
    tail = jnp.where(lines == 0, row_of(grad_power), 0.0)
    tail = jnp.where(lines == 1, row_of(feature_power), tail)
    tail = jnp.concatenate([tail, jnp.zeros((TAIL, width - nodes), jnp.float32)], axis=1)
    sent_ref[2 * nodes :, :] = tail.astype(jnp.int32).astype(jnp.int16)


def prepare(features, old_grad, w_neigh, old_degree, tables):
    nodes, width = features.shape
    slots = tables[0].shape[-1]
    args = (features, old_grad, w_neigh, old_degree, *tables)
    outs = (
        jax.ShapeDtypeStruct((2 * nodes + TAIL, width), jnp.int16),
        jax.ShapeDtypeStruct((2, slots + 8, TILE), jnp.int32),
    )

    def whole(arg):
        return pl.BlockSpec(arg.shape, lambda _: (0,) * len(arg.shape))

    return pl.pallas_call(
        prepare_kernel,
        out_shape=outs,
        grid=(1,),
        in_specs=[whole(arg) for arg in args],
        out_specs=tuple(whole(out) for out in outs),
        compiler_params=pltpu.CompilerParams(vmem_limit_bytes=VMEM),
    )(*args)


def sums_kernel(
    lane_ref,
    own_ref,
    other_ref,
    sent_ref,
    out_ref,
    infos,
    dst_rows,
    src_rows,
    counts,
    raw,
    factors,
    held,
    wide,
    sems,
):
    lane = lane_ref[0]
    devices, nodes = out_ref.shape[0] // 2, out_ref.shape[2]
    senders = raw.shape[0]
    planes = senders // 2
    slots = own_ref.shape[1] - 8
    pairs = slots // 2
    info_fetches = [
        pltpu.make_async_copy(
            table.at[1 - array, pl.ds(slots, 8)],
            infos.at[2 * array + half],
            sems.at[2 * array + half],
        )
        for array in range(2)
        for half, table in enumerate((own_ref, other_ref))
    ]
    fetch = pltpu.make_async_copy(sent_ref, raw, sems.at[4])
    for copy in info_fetches + [fetch]:
        copy.start()

    def hold(array):
        first = array * nodes
        powers = [raw[sender, 2 * nodes :, :TILE][array : array + 1] for sender in range(senders)]
        powers = [power.astype(jnp.int32).astype(jnp.float32) for power in powers]
        rest = jnp.ones((TILE - senders, TILE), jnp.float32)
        factor = jnp.concatenate([undone(jnp.concatenate(powers, axis=0)), rest], axis=0).T
        for sender in range(senders):
            factors[sender] = jnp.broadcast_to(
                factor[:nodes, sender : sender + 1], (nodes, TILE)
            )

        def move(sender, begin, into, size):
            values = raw[sender, first + begin : first + begin + size, :]
            values = values.astype(jnp.int32).astype(jnp.float32)
            times = factors[sender, begin : begin + size, :]
            times = jnp.concatenate([times] * (values.shape[1] // TILE), axis=1)
            rows = pl.ds(pl.multiple_of(into, 16), size)
            held[rows, :] = (values * times).astype(jnp.bfloat16)

        def move_plane(plane, carry):
            whole, part = plane * TILE, planes * TILE + plane * HALF
            one, two = 2 * plane, 2 * plane + 1

            @pl.when(lane == 0)
            def _():
                move(one, 0, whole, nodes)
                move(two, 0, whole + nodes, TILE - nodes)
                move(two, TILE - nodes, part, HALF)

            @pl.when(lane == 1)
            def _():
                move(one, 0, part, HALF)
                move(one, HALF, whole, nodes - HALF)
                move(two, 0, whole + nodes - HALF, nodes)

            return carry

        lax.fori_loop(0, planes, move_plane, 0)

    lanes = lax.broadcasted_iota(jnp.int32, (pairs, TILE), 1)
    left = lanes < HALF

    def plan(at, edges):
        even, odd = edges[pl.ds(0, pairs, 2), :], edges[pl.ds(1, pairs, 2), :]

        def field(at):
            return jnp.where(left, even[:, at : at + 1], odd[:, at : at + 1])

        values = jnp.where(left, even, pltpu.roll(odd, HALF, 1))
        column, count = field(HALF + 1), field(HALF + 2)
        plane = (column * 43) >> 7
        part = column - 3 * plane
        source = values & (TILE - 1)
        whole = part == 2 * lane
        own = whole | ((part == 1) & ((source >> 6) == lane))
        own &= (lanes & (HALF - 1)) < count
        place = jnp.where(whole, source, (source & (HALF - 1)) + (plane & 1) * HALF)
        place += jnp.where(left, 0, TILE)
        dst_rows[at] = jnp.where(own, values >> 7, -1).astype(jnp.float32)
        src_rows[at] = jnp.where(own, place, -1).astype(jnp.float32)
        return jnp.sum((even[:, HALF + 2 : HALF + 3] > 0).astype(jnp.int32))

    dst_ids = lax.broadcasted_iota(jnp.int32, (TILE, TILE), 0).astype(jnp.bfloat16)
    src_ids = lax.broadcasted_iota(jnp.int32, (2 * TILE, TILE), 0).astype(jnp.bfloat16)
    zero, unit = jnp.bfloat16(0), jnp.bfloat16(1)

    def spot(at, slot):
        row, column = infos[at, 0, slot], infos[at, 1, slot]
        plane = (column * 43) >> 7
        block = jnp.where(column - 3 * plane == 2 * lane, plane, planes + (plane >> 1))
        return block, pl.ds(pl.multiple_of(row * TILE, TILE), TILE)

    def pair_counts(at, pair):
        dst = dst_rows[at, pl.ds(pair, 1), :].astype(jnp.bfloat16)
        src = src_rows[at, pl.ds(pair, 1), :].astype(jnp.bfloat16)
        dst_hot = jnp.where(dst_ids == dst, unit, zero)
        src_hot = jnp.where(src_ids == src, unit, zero)
        return lax.dot_general(
            dst_hot, src_hot, (((1,), (1,)), ((), ())), preferred_element_type=jnp.float32
        ).astype(jnp.bfloat16)

    def clear(at):
        counts[at] = jnp.zeros(counts.shape[1:], jnp.bfloat16)

    def build(at, first, last, unroll):
        def add(turn, peak):
            found = [first + turn * unroll + pair for pair in range(unroll)]
            added = [pair_counts(at, pair) for pair in found]
            for pair, both in zip(found, added):
                for side in range(2):
                    block, rows = spot(at, 2 * pair + side)
                    sums = counts[at, block, rows, :]
                    sums = sums + both[:, side * TILE : (side + 1) * TILE]
                    counts[at, block, rows, :] = sums
                    peak = jnp.maximum(peak, sums)
            return peak

        start = jnp.zeros((TILE, TILE), jnp.bfloat16)
        return lax.fori_loop(0, pl.cdiv(last - first, unroll), add, start)

    def product(at):
        left_side = jnp.concatenate([counts[at, block] for block in range(counts.shape[1])], axis=1)
        return jnp.dot(left_side, held[...], preferred_element_type=jnp.float32)

    def put(array, half, sums):
        where = half + lane - 2 * half * lane
        for device in range(devices):
            rows = sums[device * nodes : (device + 1) * nodes]
            out_ref[where * devices + device, array] = rows.astype(jnp.bfloat16)

    for half in range(2):
        clear(half)
    for copy in info_fetches:
        copy.wait()
    for array in range(2):
        top = jnp.zeros((TILE, TILE), jnp.bfloat16)
        for half, edges in enumerate((own_ref, other_ref)):
            at = 2 * array + half
            live_pairs = plan(at, edges.at[1 - array])
            top = jnp.maximum(top, build(at, 0, live_pairs, UNROLL))
        top = jnp.max(top.astype(jnp.float32))
        if array == 0:
            fetch.wait()
        hold(array)

        @pl.when(top < EXACT)
        def _(array=array):
            for half in range(2):
                put(array, half, product(2 * array + half))
                if array == 0:
                    clear(2 + half)

        @pl.when(top >= EXACT)
        def _(array=array):
            for half in range(2):
                at = 2 * array + half
                wide[...] = jnp.zeros_like(wide)

                def some(turn, carry, at=at):
                    clear(at)
                    build(at, 2 * turn, 2 * turn + 2, 2)
                    wide[...] += product(at)
                    return carry

                lax.fori_loop(0, pairs // 2, some, 0)
                put(array, half, wide[...])
                if array == 0:
                    clear(2 + half)


def edge_sums(lane, own, other, sent, devices, nodes):
    slots = own.shape[1] - 8
    senders, _, width = sent.shape
    depth, rows = senders * nodes, devices * nodes
    near = pl.BlockSpec(memory_space=pltpu.VMEM)
    return pl.pallas_call(
        sums_kernel,
        out_shape=jax.ShapeDtypeStruct((2 * devices, 2, nodes, width), jnp.bfloat16),
        in_specs=[pl.BlockSpec(memory_space=pltpu.SMEM), near, near, pl.BlockSpec(memory_space=pl.ANY)],
        out_specs=near,
        scratch_shapes=[
            pltpu.SMEM((4, 8, TILE), jnp.int32),
            pltpu.VMEM((4, slots // 2, TILE), jnp.float32),
            pltpu.VMEM((4, slots // 2, TILE), jnp.float32),
            pltpu.VMEM((4, depth // TILE, rows, TILE), jnp.bfloat16),
            pltpu.VMEM(sent.shape, jnp.int16),
            pltpu.VMEM((senders, nodes, TILE), jnp.float32),
            pltpu.VMEM((depth, width), jnp.bfloat16),
            pltpu.VMEM((rows, width), jnp.float32),
            pltpu.SemaphoreType.DMA((5,)),
        ],
        compiler_params=pltpu.CompilerParams(vmem_limit_bytes=NEAR),
        cost_estimate=pl.CostEstimate(
            flops=16 * 10**9, bytes_accessed=20 * 10**6, transcendentals=0
        ),
    )(lane, own, other, sent)


def finish_kernel(
    parts,
    features,
    grad,
    w_self,
    w_neigh,
    bias_ref,
    degree_ref,
    out_ref,
    grad_out_ref,
    own_grad,
    mean,
):
    senders = parts.shape[0]
    degree = column_of(degree_ref[...].astype(jnp.float32))
    own_grad[...] = lax.dot_general(
        grad[...], w_self[...], (((1,), (1,)), ((), ())), preferred_element_type=jnp.float32
    )
    for begin in range(0, features.shape[0], 16):
        rows = pl.ds(begin, 16)

        def summed(array):
            return sum(parts[at, array, rows, :].astype(jnp.float32) for at in range(senders))

        mean[rows, :] = (summed(1) / degree[begin : begin + 16]).astype(jnp.bfloat16)
        grad_out_ref[rows, :] = (own_grad[rows, :] + summed(0)).astype(jnp.bfloat16)
    preact = jnp.dot(features[...], w_self[...], preferred_element_type=jnp.float32)
    preact = preact + jnp.dot(mean[...], w_neigh[...], preferred_element_type=jnp.float32)
    out_ref[...] = jnp.maximum(preact + bias_ref[...], 0.0).astype(jnp.bfloat16)


def finish(parts, features, old_grad, w_self, w_neigh, bias_term, degree):
    out = jax.ShapeDtypeStruct(features.shape, jnp.bfloat16)
    return pl.pallas_call(
        finish_kernel,
        out_shape=(out, out),
        scratch_shapes=[
            pltpu.VMEM(features.shape, jnp.float32),
            pltpu.VMEM(features.shape, jnp.bfloat16),
        ],
        compiler_params=pltpu.CompilerParams(vmem_limit_bytes=16 * 1024 * 1024),
    )(parts, features, old_grad, w_self, w_neigh, bias_term, degree)


def shards(
    features,
    degree,
    w_self,
    w_neigh,
    bias_term,
    tile_index,
    tile_edges,
    old_grad,
    old_degree,
    old_index,
    old_edges,
):
    nodes, width = features.shape
    devices = lax.axis_size("y") * lax.axis_size("xh")
    lane = lax.axis_index("xl")

    tables = []
    for index, edges in ((tile_index, tile_edges), (old_index, old_edges)):
        tables.append(jnp.transpose(index[0], (2, 0, 1)))
        tables.append(edges[0, 0].T)
    sent, own = prepare(features, old_grad, w_neigh, old_degree[None], tables)
    other = lax.ppermute(own, "xl", [(0, 1), (1, 0)])

    got = lax.all_gather(sent, ("z", "core"), axis=0, tiled=False)

    partial = edge_sums(lane.reshape(1), own, other, got, devices, nodes)
    parts = lax.all_to_all(partial, PLANE, 0, 0)
    return finish(parts, features, old_grad, w_self, w_neigh, bias_term[None], degree[None])


def solution(mesh):
    parts = Mesh(mesh.devices.reshape(16, 2, 2, 4, 2), PARTS)
    block = ("z", "xl", "core")
    side = ("y", "xh")
    in_specs = (
        P(PARTS, None),
        P(PARTS),
        P(),
        P(),
        P(),
        P(block, side, None, None),
        P(block, side, None, None),
        P(PARTS, None),
        P(PARTS),
        P(block, side, None, None),
        P(block, side, None, None),
    )
    out_specs = (P(PARTS, None), P(PARTS, None))
    return jax.shard_map(
        shards, mesh=parts, in_specs=in_specs, out_specs=out_specs, check_vma=False
    )
```

```python
import jax
import jax.numpy as jnp
from jax import lax
from jax.experimental import pallas as pl
from jax.experimental.pallas import tpu as pltpu
from jax.sharding import Mesh
from jax.sharding import PartitionSpec as P

TILE = 128
HALF = TILE // 2
UNROLL = 12
EXACT = 256
VMEM = 58 * 1024 * 1024
NEAR = 52 * 1024 * 1024
PARTS = ("z", "xl", "core", "y", "xh")
PLANE = ("xl", "y", "xh")
SHIFTS = (63, 32, 16, 8, 4, 2, 1)
LARGEST = 32767.0
TAIL = 16


def column_of(row):
    count = row.shape[1]
    across = lax.broadcasted_iota(jnp.int32, (count, count), 0)
    down = lax.broadcasted_iota(jnp.int32, (count, count), 1)
    return jnp.sum(jnp.where(across == down, row, 0.0), axis=1, keepdims=True)


def row_of(column):
    count = column.shape[0]
    across = lax.broadcasted_iota(jnp.int32, (count, count), 0)
    down = lax.broadcasted_iota(jnp.int32, (count, count), 1)
    return jnp.sum(jnp.where(across == down, column, 0.0), axis=0, keepdims=True)


def scaled(values):
    top = jnp.max(jnp.abs(values), axis=1, keepdims=True)
    scale, power = jnp.ones_like(top), jnp.zeros_like(top)
    for shift in SHIFTS:
        fits = top * 2.0**shift <= LARGEST
        factor = jnp.where(fits, 2.0**shift, 1.0)
        top, scale = top * factor, scale * factor
        power += jnp.where(fits, float(shift), 0.0)
    return jnp.round(values * scale).astype(jnp.int32).astype(jnp.int16), power


def undone(power):
    factor = jnp.ones_like(power)
    for shift in SHIFTS:
        has = power >= shift
        factor = factor * jnp.where(has, 2.0**-shift, 1.0)
        power = power - jnp.where(has, float(shift), 0.0)
    return factor


def prepare_kernel(
    features_ref,
    grad_ref,
    weight_ref,
    degree_ref,
    index_ref,
    edges_ref,
    old_index_ref,
    old_edges_ref,
    sent_ref,
    slots_ref,
):
    nodes, width = grad_ref.shape
    for at, (index, edges) in enumerate(
        ((index_ref, edges_ref), (old_index_ref, old_edges_ref))
    ):
        fields, _, slots = index.shape
        numbers = jnp.concatenate([edges[...]] + [index[field] for field in range(fields)], axis=0)
        numbers = jnp.concatenate(
            [numbers, jnp.zeros((TILE - HALF - fields, slots), jnp.int32)], axis=0
        )
        numbers = jnp.concatenate(
            [numbers, jnp.zeros((TILE, TILE - slots), jnp.int32)], axis=1
        )
        slots_ref[at, :slots, :] = numbers.astype(jnp.float32).T[:slots].astype(jnp.int32)
        slots_ref[at, slots:, :] = numbers[HALF : HALF + 8, :]

    product = lax.dot_general(
        grad_ref[...],
        weight_ref[...],
        (((1,), (1,)), ((), ())),
        preferred_element_type=jnp.float32,
    )
    degree = column_of(degree_ref[...].astype(jnp.float32))
    mean_grad = (product / degree).astype(jnp.bfloat16).astype(jnp.float32)
    values, grad_power = scaled(mean_grad)
    sent_ref[:nodes, :] = values
    values, feature_power = scaled(features_ref[...].astype(jnp.float32))
    sent_ref[nodes : 2 * nodes, :] = values
    lines = lax.broadcasted_iota(jnp.int32, (TAIL, nodes), 0)
    tail = jnp.where(lines == 0, row_of(grad_power), 0.0)
    tail = jnp.where(lines == 1, row_of(feature_power), tail)
    tail = jnp.concatenate([tail, jnp.zeros((TAIL, width - nodes), jnp.float32)], axis=1)
    sent_ref[2 * nodes :, :] = tail.astype(jnp.int32).astype(jnp.int16)


def prepare(features, old_grad, w_neigh, old_degree, tables):
    nodes, width = features.shape
    slots = tables[0].shape[-1]
    args = (features, old_grad, w_neigh, old_degree, *tables)
    outs = (
        jax.ShapeDtypeStruct((2 * nodes + TAIL, width), jnp.int16),
        jax.ShapeDtypeStruct((2, slots + 8, TILE), jnp.int32),
    )

    def whole(arg):
        return pl.BlockSpec(arg.shape, lambda _: (0,) * len(arg.shape))

    return pl.pallas_call(
        prepare_kernel,
        out_shape=outs,
        grid=(1,),
        in_specs=[whole(arg) for arg in args],
        out_specs=tuple(whole(out) for out in outs),
        compiler_params=pltpu.CompilerParams(vmem_limit_bytes=VMEM),
    )(*args)


def sums_kernel(
    lane_ref,
    own_ref,
    other_ref,
    sent_ref,
    out_ref,
    infos,
    dst_rows,
    src_rows,
    counts,
    raw,
    factors,
    held,
    wide,
    sems,
):
    lane = lane_ref[0]
    devices, nodes = out_ref.shape[0] // 2, out_ref.shape[2]
    senders = raw.shape[0]
    planes = senders // 2
    slots = own_ref.shape[1] - 8
    pairs = slots // 2
    info_fetches = [
        pltpu.make_async_copy(
            table.at[1 - array, pl.ds(slots, 8)],
            infos.at[2 * array + half],
            sems.at[2 * array + half],
        )
        for array in range(2)
        for half, table in enumerate((own_ref, other_ref))
    ]
    fetch = pltpu.make_async_copy(sent_ref, raw, sems.at[4])
    for copy in info_fetches + [fetch]:
        copy.start()

    def hold(array):
        first = array * nodes
        powers = [raw[sender, 2 * nodes :, :TILE][array : array + 1] for sender in range(senders)]
        powers = [power.astype(jnp.int32).astype(jnp.float32) for power in powers]
        rest = jnp.ones((TILE - senders, TILE), jnp.float32)
        factor = jnp.concatenate([undone(jnp.concatenate(powers, axis=0)), rest], axis=0).T
        for sender in range(senders):
            factors[sender] = jnp.broadcast_to(
                factor[:nodes, sender : sender + 1], (nodes, TILE)
            )

        def move(sender, begin, into, size):
            values = raw[sender, first + begin : first + begin + size, :]
            values = values.astype(jnp.int32).astype(jnp.float32)
            times = factors[sender, begin : begin + size, :]
            times = jnp.concatenate([times] * (values.shape[1] // TILE), axis=1)
            rows = pl.ds(pl.multiple_of(into, 16), size)
            held[rows, :] = (values * times).astype(jnp.bfloat16)

        def move_plane(plane, carry):
            whole, part = plane * TILE, planes * TILE + plane * HALF
            one, two = 2 * plane, 2 * plane + 1

            @pl.when(lane == 0)
            def _():
                move(one, 0, whole, nodes)
                move(two, 0, whole + nodes, TILE - nodes)
                move(two, TILE - nodes, part, HALF)

            @pl.when(lane == 1)
            def _():
                move(one, 0, part, HALF)
                move(one, HALF, whole, nodes - HALF)
                move(two, 0, whole + nodes - HALF, nodes)

            return carry

        lax.fori_loop(0, planes, move_plane, 0)

    lanes = lax.broadcasted_iota(jnp.int32, (pairs, TILE), 1)
    left = lanes < HALF

    def plan(at, edges):
        even, odd = edges[pl.ds(0, pairs, 2), :], edges[pl.ds(1, pairs, 2), :]

        def field(at):
            return jnp.where(left, even[:, at : at + 1], odd[:, at : at + 1])

        values = jnp.where(left, even, pltpu.roll(odd, HALF, 1))
        column, count = field(HALF + 1), field(HALF + 2)
        plane = (column * 43) >> 7
        part = column - 3 * plane
        source = values & (TILE - 1)
        whole = part == 2 * lane
        own = whole | ((part == 1) & ((source >> 6) == lane))
        own &= (lanes & (HALF - 1)) < count
        place = jnp.where(whole, source, (source & (HALF - 1)) + (plane & 1) * HALF)
        place += jnp.where(left, 0, TILE)
        dst_rows[at] = jnp.where(own, values >> 7, -1).astype(jnp.float32)
        src_rows[at] = jnp.where(own, place, -1).astype(jnp.float32)
        return jnp.sum((even[:, HALF + 2 : HALF + 3] > 0).astype(jnp.int32))

    dst_ids = lax.broadcasted_iota(jnp.int32, (TILE, TILE), 0).astype(jnp.bfloat16)
    src_ids = lax.broadcasted_iota(jnp.int32, (2 * TILE, TILE), 0).astype(jnp.bfloat16)
    zero, unit = jnp.bfloat16(0), jnp.bfloat16(1)

    def spot(at, slot):
        row, column = infos[at, 0, slot], infos[at, 1, slot]
        plane = (column * 43) >> 7
        block = jnp.where(column - 3 * plane == 2 * lane, plane, planes + (plane >> 1))
        return block, pl.ds(pl.multiple_of(row * TILE, TILE), TILE)

    def pair_counts(at, pair):
        dst = dst_rows[at, pl.ds(pair, 1), :].astype(jnp.bfloat16)
        src = src_rows[at, pl.ds(pair, 1), :].astype(jnp.bfloat16)
        dst_hot = jnp.where(dst_ids == dst, unit, zero)
        src_hot = jnp.where(src_ids == src, unit, zero)
        return lax.dot_general(
            dst_hot, src_hot, (((1,), (1,)), ((), ())), preferred_element_type=jnp.float32
        ).astype(jnp.bfloat16)

    def clear(at):
        counts[at] = jnp.zeros(counts.shape[1:], jnp.bfloat16)

    def build(at, first, last, unroll):
        def add(turn, peak):
            found = [first + turn * unroll + pair for pair in range(unroll)]
            added = [pair_counts(at, pair) for pair in found]
            for pair, both in zip(found, added):
                for side in range(2):
                    block, rows = spot(at, 2 * pair + side)
                    sums = counts[at, block, rows, :]
                    sums = sums + both[:, side * TILE : (side + 1) * TILE]
                    counts[at, block, rows, :] = sums
                    peak = jnp.maximum(peak, sums)
            return peak

        start = jnp.zeros((TILE, TILE), jnp.bfloat16)
        return lax.fori_loop(0, pl.cdiv(last - first, unroll), add, start)

    def product(at):
        left_side = jnp.concatenate([counts[at, block] for block in range(counts.shape[1])], axis=1)
        return jnp.dot(left_side, held[...], preferred_element_type=jnp.float32)

    def put(array, half, sums):
        where = half + lane - 2 * half * lane
        for device in range(devices):
            rows = sums[device * nodes : (device + 1) * nodes]
            out_ref[where * devices + device, array] = rows.astype(jnp.bfloat16)

    for half in range(2):
        clear(half)
    for copy in info_fetches:
        copy.wait()
    for array in range(2):
        top = jnp.zeros((TILE, TILE), jnp.bfloat16)
        for half, edges in enumerate((own_ref, other_ref)):
            at = 2 * array + half
            live_pairs = plan(at, edges.at[1 - array])
            top = jnp.maximum(top, build(at, 0, live_pairs, UNROLL))
        top = jnp.max(top.astype(jnp.float32))
        if array == 0:
            fetch.wait()
        hold(array)

        @pl.when(top < EXACT)
        def _(array=array):
            for half in range(2):
                put(array, half, product(2 * array + half))
                if array == 0:
                    clear(2 + half)

        @pl.when(top >= EXACT)
        def _(array=array):
            for half in range(2):
                at = 2 * array + half
                wide[...] = jnp.zeros_like(wide)

                def some(turn, carry, at=at):
                    clear(at)
                    build(at, 2 * turn, 2 * turn + 2, 2)
                    wide[...] += product(at)
                    return carry

                lax.fori_loop(0, pairs // 2, some, 0)
                put(array, half, wide[...])
                if array == 0:
                    clear(2 + half)


def edge_sums(lane, own, other, sent, devices, nodes):
    slots = own.shape[1] - 8
    senders, _, width = sent.shape
    depth, rows = senders * nodes, devices * nodes
    near = pl.BlockSpec(memory_space=pltpu.VMEM)
    return pl.pallas_call(
        sums_kernel,
        out_shape=jax.ShapeDtypeStruct((2 * devices, 2, nodes, width), jnp.bfloat16),
        in_specs=[pl.BlockSpec(memory_space=pltpu.SMEM), near, near, pl.BlockSpec(memory_space=pl.ANY)],
        out_specs=near,
        scratch_shapes=[
            pltpu.SMEM((4, 8, TILE), jnp.int32),
            pltpu.VMEM((4, slots // 2, TILE), jnp.float32),
            pltpu.VMEM((4, slots // 2, TILE), jnp.float32),
            pltpu.VMEM((4, depth // TILE, rows, TILE), jnp.bfloat16),
            pltpu.VMEM(sent.shape, jnp.int16),
            pltpu.VMEM((senders, nodes, TILE), jnp.float32),
            pltpu.VMEM((depth, width), jnp.bfloat16),
            pltpu.VMEM((rows, width), jnp.float32),
            pltpu.SemaphoreType.DMA((5,)),
        ],
        compiler_params=pltpu.CompilerParams(vmem_limit_bytes=NEAR),
        cost_estimate=pl.CostEstimate(
            flops=16 * 10**9, bytes_accessed=20 * 10**6, transcendentals=0
        ),
    )(lane, own, other, sent)


def finish_kernel(
    parts,
    features,
    grad,
    w_self,
    w_neigh,
    bias_ref,
    degree_ref,
    out_ref,
    grad_out_ref,
    own_grad,
    mean,
):
    senders = parts.shape[0]
    degree = column_of(degree_ref[...].astype(jnp.float32))
    own_grad[...] = lax.dot_general(
        grad[...], w_self[...], (((1,), (1,)), ((), ())), preferred_element_type=jnp.float32
    )
    for begin in range(0, features.shape[0], 16):
        rows = pl.ds(begin, 16)

        def summed(array):
            return sum(parts[at, array, rows, :].astype(jnp.float32) for at in range(senders))

        mean[rows, :] = (summed(1) / degree[begin : begin + 16]).astype(jnp.bfloat16)
        grad_out_ref[rows, :] = (own_grad[rows, :] + summed(0)).astype(jnp.bfloat16)
    preact = jnp.dot(features[...], w_self[...], preferred_element_type=jnp.float32)
    preact = preact + jnp.dot(mean[...], w_neigh[...], preferred_element_type=jnp.float32)
    out_ref[...] = jnp.maximum(preact + bias_ref[...], 0.0).astype(jnp.bfloat16)


def finish(parts, features, old_grad, w_self, w_neigh, bias_term, degree):
    out = jax.ShapeDtypeStruct(features.shape, jnp.bfloat16)
    return pl.pallas_call(
        finish_kernel,
        out_shape=(out, out),
        scratch_shapes=[
            pltpu.VMEM(features.shape, jnp.float32),
            pltpu.VMEM(features.shape, jnp.bfloat16),
        ],
        compiler_params=pltpu.CompilerParams(vmem_limit_bytes=16 * 1024 * 1024),
    )(parts, features, old_grad, w_self, w_neigh, bias_term, degree)


def shards(
    features,
    degree,
    w_self,
    w_neigh,
    bias_term,
    tile_index,
    tile_edges,
    old_grad,
    old_degree,
    old_index,
    old_edges,
):
    nodes, width = features.shape
    devices = lax.axis_size("y") * lax.axis_size("xh")
    lane = lax.axis_index("xl")

    tables = []
    for index, edges in ((tile_index, tile_edges), (old_index, old_edges)):
        tables.append(jnp.transpose(index[0], (2, 0, 1)))
        tables.append(edges[0, 0].T)
    sent, own = prepare(features, old_grad, w_neigh, old_degree[None], tables)
    other = lax.ppermute(own, "xl", [(0, 1), (1, 0)])

    got = lax.all_gather(sent, ("z", "core"), axis=0, tiled=False)

    partial = edge_sums(lane.reshape(1), own, other, got, devices, nodes)
    parts = lax.all_to_all(partial, PLANE, 0, 0)
    return finish(parts, features, old_grad, w_self, w_neigh, bias_term[None], degree[None])


def solution(mesh):
    parts = Mesh(mesh.devices.reshape(16, 2, 2, 4, 2), PARTS)
    block = ("z", "xl", "core")
    side = ("y", "xh")
    in_specs = (
        P(PARTS, None),
        P(PARTS),
        P(),
        P(),
        P(),
        P(block, side, None, None),
        P(block, side, None, None),
        P(PARTS, None),
        P(PARTS),
        P(block, side, None, None),
        P(block, side, None, None),
    )
    out_specs = (P(PARTS, None), P(PARTS, None))
    return jax.shard_map(
        shards, mesh=parts, in_specs=in_specs, out_specs=out_specs, check_vma=False
    )
```
